32 devices in a mesh: groups: 2 (over y), inst: 4 (over z), tp: 4 (over x, core).
Axes of the slice: x: 2, y: 2, z: 4, core: 2. Of those that a mesh axis runs over, the one named last changes fastest.
Arguments:
- token_hidden_input: bfloat16 [512, 8192], P(('groups', 'inst'), 'tp'), parts along dimension 0, may hold values from -6 to 6
- base_query_rows: bfloat16 [512, 8192], P(('groups', 'inst'), 'tp'), parts along dimension 0, may hold values from -5 to 5
- token_key: bfloat16 [512, 1024], P(('groups', 'inst'), 'tp'), parts along dimension 0, may hold values from -5 to 5
- token_value: bfloat16 [512, 1024], P(('groups', 'inst'), 'tp'), parts along dimension 0, may hold values from -5 to 5
- cached_key_rows: bfloat16 [512, 8, 64, 128], P(('groups', 'inst'), 'tp'), parts along dimension 0, may hold values from -5 to 5
- cached_value_rows: bfloat16 [512, 8, 64, 128], P(('groups', 'inst'), 'tp'), parts along dimension 0, may hold values from -5 to 5
- request_cache_length: int32 [512], P(('groups', 'inst')), parts along dimension 0, may hold values from 1 to 64, as said below
- request_adapter: int32 [512], P(('groups', 'inst')), parts along dimension 0, may hold values from 0 to 31, as said below
- adapter_storage_row: int32 [64], P('groups'), parts along dimension 0, may hold values from 0 to 31, as said below
- adapter_down_weight: bfloat16 [64, 8192, 64], P(('groups', 'inst'), 'tp'), parts along dimension 0, may hold values from -0.0625 to 0.0625
- adapter_up_weight: bfloat16 [64, 64, 8192], P(('groups', 'inst'), None, 'tp'), parts along dimension 0, may hold values from -0.75 to 0.75
Outputs:
- attended: bfloat16 [512, 8192], P(('groups', 'inst'), 'tp'), parts along dimension 0
The draws below stay inside these ranges and needn't reach their ends.
There are 2 independent parts, one for each index of `groups`. The reference program is written for one: setup_inputs(seed, part) draws one part's arguments, and reference() takes and returns one part's arrays. A program takes and returns all parts, laid end to end along the dimension named above; each array names one. Nothing has to cross between parts.
Inputs may be any that keep to these rules, and one draw needn't show every extreme that they name: `adapter_storage_row`: storage row s lies on instance s // 8 as row s % 8 there; every row is named once. `request_adapter`: in each aligned block of 64 requests (one instance's), at most 32 requests have their adapter's storage row on one instance, and exactly 32 do for some instance. `request_cache_length`: some request has exactly 64 filled slots.
All inputs are finite; a program needn't handle non-finite values.
Results may differ from the reference program's by a relative error of at most 0.0066.
Values may be sent and summed in bfloat16 or wider, within the bound.
A program may use at most 64 MiB of HBM per device.

```python
import jax
import jax.numpy as jnp
from jax import lax

MODEL_WIDTH = 8192
KVH = 8
HD = 128
ADAPTER_RANK = 64
REQ_INST = 64
L = 64
ADP_DEV = 8
GROUP = 8
QUERY_FEATURES = 8192
REQUESTS = 256
ADAPTER_COUNT = 32
CAP = 32


def storage_order(key):
    return jax.random.permutation(jax.random.fold_in(key, 202), ADAPTER_COUNT).astype(jnp.int32)


def draw_base_query_rows(key, part):
    key = jax.random.fold_in(key, 1)
    base = jnp.clip(jax.random.normal(key, (REQUESTS, KVH, GROUP, HD), jnp.float32), -5.0, 5.0)
    return base.reshape(REQUESTS, QUERY_FEATURES).astype(jnp.bfloat16)


def draw_cached_key_rows(key, part):
    key = jax.random.fold_in(key, 2)
    base = jnp.clip(jax.random.normal(key, (REQUESTS, KVH, L, HD), jnp.float32), -5.0, 5.0)
    return base.astype(jnp.bfloat16)


def draw_request_cache_length(key, part):
    key = jax.random.fold_in(key, 3)
    k_len, k_pick = jax.random.split(key)
    lengths = jax.random.randint(k_len, (REQUESTS,), 1, L + 1)
    picked = jax.random.randint(k_pick, (), 0, REQUESTS)
    return jnp.where(jnp.arange(REQUESTS) == picked, L, lengths).astype(jnp.int32)


def draw_adapter_storage_row(key, part):
    order = storage_order(key)
    return order


def draw_request_adapter(key, part):
    order = storage_order(key)
    key = jax.random.fold_in(key, 5)
    k_home, k_coin, k_mix, k_local = jax.random.split(key, 4)
    blocks = REQUESTS // REQ_INST
    owners = ADAPTER_COUNT // ADP_DEV
    homes = jax.vmap(lambda k: jax.random.permutation(k, owners))(jax.random.split(k_home, blocks))
    places = jnp.arange(REQ_INST)
    coin = jax.random.randint(k_coin, (blocks, REQ_INST), 0, 2)
    bucket = jnp.where(places[None, :] < CAP, 0, 1 + 2 * ((places[None, :] - CAP) // CAP) + coin)
    mixing = jax.vmap(lambda k: jax.random.permutation(k, REQ_INST))(jax.random.split(k_mix, blocks))
    bucket = jnp.take_along_axis(bucket, mixing, axis=1)
    home = jnp.take_along_axis(homes, bucket, axis=1)
    local = jax.random.randint(k_local, (blocks, REQ_INST), 0, ADP_DEV)
    slots = (home * ADP_DEV + local).reshape(-1)
    inverse = jnp.argsort(order).astype(jnp.int32)
    return inverse[slots].astype(jnp.int32)


def shard_levels(stream_key, extent, cuts, least, high):
    level = 1.0
    for position, parts in cuts:
        steps = jax.random.uniform(jax.random.fold_in(jax.random.fold_in(stream_key, 6), position), (parts,), jnp.float32, least / len(cuts), high / len(cuts))
        level = level * jnp.repeat(jnp.exp(steps), extent[position] // parts).reshape((-1,) + (1,) * (len(extent) - 1 - position))
    return level


def scatter_about(key, dims, spread, bound, cuts=(), kind=jnp.bfloat16):
    level = shard_levels(key, dims, cuts, -0.22, 0.18) if cuts else 1.0
    values = jax.random.normal(key, dims, jnp.float32) * spread * level
    return jnp.minimum(jnp.maximum(values, -bound), bound).astype(kind)


def setup_inputs(seed: int = 0, part: int = 0) -> dict:
    key_of = jax.random.split(jax.random.key(seed), 12)
    own_keys = jax.random.split(jax.random.fold_in(key_of[11], part), 12)
    return {
        "token_hidden_input": scatter_about(own_keys[0], (REQUESTS, MODEL_WIDTH), 1.0, 6.0, ((0, 4), (1, 4))),
        "base_query_rows": draw_base_query_rows(jax.random.fold_in(jax.random.fold_in(key_of[11], part), 71), part),
        "token_key": scatter_about(own_keys[2], (REQUESTS, KVH * HD), 1.0, 5.0, ((0, 4), (1, 4))),
        "token_value": scatter_about(own_keys[3], (REQUESTS, KVH * HD), 1.0, 5.0, ((0, 4), (1, 4))),
        "cached_key_rows": draw_cached_key_rows(jax.random.fold_in(jax.random.fold_in(key_of[11], part), 71), part),
        "cached_value_rows": scatter_about(own_keys[5], (REQUESTS, KVH, L, HD), 1.0, 5.0, ((0, 4), (1, 4))),
        "request_cache_length": draw_request_cache_length(jax.random.fold_in(jax.random.fold_in(key_of[11], part), 71), part),
        "request_adapter": draw_request_adapter(jax.random.fold_in(jax.random.fold_in(key_of[11], part), 71), part),
        "adapter_storage_row": draw_adapter_storage_row(jax.random.fold_in(jax.random.fold_in(key_of[11], part), 71), part),
        "adapter_down_weight": scatter_about(own_keys[9], (ADAPTER_COUNT, MODEL_WIDTH, ADAPTER_RANK), MODEL_WIDTH ** -0.5, 0.0625, ((0, 4), (1, 4))),
        "adapter_up_weight": scatter_about(own_keys[10], (ADAPTER_COUNT, ADAPTER_RANK, QUERY_FEATURES), ADAPTER_RANK ** -0.5, 0.75, ((0, 4), (2, 4))),
    }


def attend_block(query, token_key, token_value, cached_key_rows, cached_value_rows, lengths):
    rows = query.shape[0]
    scale = HD ** -0.5
    q4 = query.reshape(rows, KVH, GROUP, HD).astype(jnp.float32)
    scores = jnp.einsum('bgjh,bglh->bgjl', q4, cached_key_rows.astype(jnp.float32)) * scale
    valid = jnp.arange(L, dtype=jnp.int32)[None, :] < lengths[:, None]
    scores = jnp.where(valid[:, None, None, :], scores, -1e30)
    fresh_key = token_key.reshape(rows, KVH, HD).astype(jnp.float32)
    fresh = jnp.einsum('bgjh,bgh->bgj', q4, fresh_key) * scale
    top = jnp.maximum(jnp.max(scores, axis=-1), fresh)
    expo = jnp.exp(scores - top[..., None])
    expo_new = jnp.exp(fresh - top)
    total = jnp.sum(expo, axis=-1) + expo_new
    weights = (expo / total[..., None]).astype(jnp.bfloat16)
    weight_new = (expo_new / total).astype(jnp.bfloat16)
    fresh_value = token_value.reshape(rows, KVH, HD).astype(jnp.float32)
    out = jnp.einsum('bgjl,bglh->bgjh', weights.astype(jnp.float32), cached_value_rows.astype(jnp.float32))
    out = out + weight_new.astype(jnp.float32)[..., None] * fresh_value[:, :, None, :]
    return out.reshape(rows, QUERY_FEATURES).astype(jnp.bfloat16)


def reference(token_hidden_input, base_query_rows, token_key, token_value, cached_key_rows, cached_value_rows, request_cache_length, request_adapter, adapter_storage_row, adapter_down_weight, adapter_up_weight):
    slot = adapter_storage_row[request_adapter].astype(jnp.int32)
    blocks = REQUESTS // REQ_INST

    def one_block(pieces):
        x, base, knew, vnew, kc, vc, lengths, storage_row_index = pieces
        down_product = adapter_down_weight[storage_row_index].astype(jnp.float32)
        low = jnp.einsum('bd,bdr->br', x.astype(jnp.float32), down_product).astype(jnp.bfloat16)
        up_product = adapter_up_weight[storage_row_index].astype(jnp.float32)
        query_update = jnp.einsum('br,brq->bq', low.astype(jnp.float32), up_product).astype(jnp.bfloat16)
        query = (base.astype(jnp.float32) + query_update.astype(jnp.float32)).astype(jnp.bfloat16)
        return attend_block(query, knew, vnew, kc, vc, lengths)

    def split(a):
        return a.reshape((blocks, REQ_INST) + a.shape[1:])

    pieces = (split(token_hidden_input), split(base_query_rows), split(token_key), split(token_value), split(cached_key_rows), split(cached_value_rows), split(request_cache_length), split(slot))
    out = lax.map(one_block, pieces)
    return out.reshape(REQUESTS, QUERY_FEATURES)
```

```python
import functools

import jax
import jax.numpy as jnp
from jax import lax
from jax.experimental import pallas as pl
from jax.experimental.pallas import tpu as pltpu
from jax.sharding import PartitionSpec as P

MESH = pl.DeviceIdType.MESH
F32 = jnp.float32
BF16 = jnp.bfloat16
TILE = 16
BLOCK = 8


def iota(shape, axis):
    return lax.broadcasted_iota(jnp.int32, shape, axis)


def to_column(row, count):
    shape = (count, row.shape[1])
    return jnp.sum(jnp.where(iota(shape, 0) == iota(shape, 1), row, 0.0), axis=1, keepdims=True)


def to_row(column):
    n = column.shape[0]
    return jnp.sum(jnp.where(iota((n, n), 0) == iota((n, n), 1), column, 0.0), axis=0, keepdims=True)


def kernel(
    owners, shards, chunks,
    adapter_ref, storage_ref, length_ref,
    x_hbm, base_hbm, tk_hbm, tv_hbm, k_hbm, v_hbm, down_hbm, up_hbm,
    out_ref,
    x, base, tk, tv, kbuf, vbuf, down, up,
    snd, arr, tag_snd, tag_arr, part, delta, ret,
    in_sem, snd_send, snd_recv, tag_send, tag_recv, part_send, part_recv, ret_send, ret_recv,
):
    me = lax.axis_index("inst")
    tp = lax.axis_index("tp")
    requests, width = x.shape
    heads = kbuf.shape[0]
    slots, head = kbuf.shape[2], kbuf.shape[3]
    span = width // heads
    group = span // head
    lanes = down.shape[0]
    rank = 64
    kept = lanes // rank
    rows = owners * TILE
    peer = lambda j: {"inst": lax.rem(me + j, owners)}
    mate = lambda j: {"tp": lax.rem(tp + j, shards)}

    loads = [pltpu.make_async_copy(x_hbm, x, in_sem.at[0])]
    loads.append(pltpu.make_async_copy(down_hbm, down, in_sem.at[1]))
    loads.append(pltpu.make_async_copy(up_hbm, up, in_sem.at[2]))
    loads.append(pltpu.make_async_copy(base_hbm, base, in_sem.at[3]))
    loads.append(pltpu.make_async_copy(tk_hbm, tk, in_sem.at[4]))
    loads.append(pltpu.make_async_copy(tv_hbm, tv, in_sem.at[5]))
    for g in range(heads):
        loads.append(pltpu.make_async_copy(k_hbm.at[:, g], kbuf.at[g], in_sem.at[6 + 2 * g]))
        loads.append(pltpu.make_async_copy(v_hbm.at[:, g], vbuf.at[g], in_sem.at[7 + 2 * g]))
    for load in loads:
        load.start()

    barrier = pltpu.get_barrier_semaphore()
    for j in range(1, owners):
        pl.semaphore_signal(barrier, inc=1, device_id=peer(j), device_id_type=MESH)
    for j in range(1, shards):
        pl.semaphore_signal(barrier, inc=1, device_id=mate(j), device_id_type=MESH)

    catalog = storage_ref.shape[1]
    adapter = to_column(adapter_ref[...].astype(F32), requests)
    stored = storage_ref[...].astype(F32)
    slot = jnp.sum(
        jnp.where(adapter == iota((requests, catalog), 1).astype(F32), stored, 0.0), axis=1, keepdims=True
    )
    home = jnp.floor((slot + 0.5) * (1.0 / kept))
    tag = slot - home * kept + 1.0
    home = home - me.astype(F32)
    home = jnp.where(home < 0.0, home + owners, home)
    home_row = to_row(home)
    square = (requests, requests)
    earlier = (home == home_row) & (iota(square, 1) < iota(square, 0))
    place = jnp.sum(jnp.where(earlier, 1.0, 0.0), axis=1, keepdims=True)
    turn = jnp.floor((place + 0.5) * (1.0 / TILE))
    spot = turn * rows + home * TILE + (place - turn * TILE)
    spot_row = to_row(spot)

    for j in range(owners):
        shape = (requests, 128)
        here = (home == float(j)) & (place == iota(shape, 1).astype(F32))
        line = jnp.sum(jnp.where(here, tag, 0.0), axis=0, keepdims=True)
        if j:
            tag_snd[j] = jnp.broadcast_to(line, (8, 128))
        else:
            tag_arr[0] = jnp.broadcast_to(line, (8, 128))

    loads[0].wait()
    own = []
    order = sorted(range(1, owners), key=lambda j: (abs(2 * j - owners), j))
    sends = []
    for c in range(chunks):
        placing = (iota((rows, requests), 0).astype(F32) + float(c * rows) == spot_row)
        packed = jnp.dot(placing.astype(F32).astype(BF16), x[...], preferred_element_type=F32).astype(BF16)
        arr[c, 0] = packed[:TILE]
        snd[c] = packed.reshape(owners, TILE, width)
        if c == 0:
            pl.semaphore_wait(barrier, owners - 1 + shards - 1)
            for j in order:
                sends.append(pltpu.make_async_remote_copy(
                    src_ref=tag_snd.at[j], dst_ref=tag_arr.at[owners - j],
                    send_sem=tag_send.at[j], recv_sem=tag_recv.at[owners - j],
                    device_id=peer(j), device_id_type=MESH))
                sends[-1].start()
        for j in order:
            sends.append(pltpu.make_async_remote_copy(
                src_ref=snd.at[c, j], dst_ref=arr.at[c, owners - j],
                send_sem=snd_send.at[c, j], recv_sem=snd_recv.at[c, owners - j],
                device_id=peer(j), device_id_type=MESH))
            sends[-1].start()

    def arrived(dst, sem, j, device):
        pltpu.make_async_remote_copy(
            src_ref=dst, dst_ref=dst, send_sem=sem, recv_sem=sem,
            device_id=device, device_id_type=MESH).wait_recv()

    half = rows // 2
    which = iota((rows, lanes), 1) // rank
    left = iota((half, 128), 1) < rank
    tags = []
    for c in range(chunks):
        if c == 0:
            for j in range(1, owners):
                arrived(tag_arr.at[j], tag_recv.at[j], j, peer(j))
            loads[1].wait()
        columns = []
        for j in range(owners):
            shape = (TILE, 128)
            match = iota(shape, 1) == iota(shape, 0) + c * TILE
            columns.append(jnp.sum(jnp.where(match, tag_arr[j, 0:1, :], 0.0), axis=1, keepdims=True))
        mine = which.astype(F32) == jnp.concatenate(columns, axis=0) - 1.0
        tags.append(mine)
        for j in range(1, owners):
            arrived(arr.at[c, j], snd_recv.at[c, j], j, peer(j))
        product = lax.dot_general(
            arr[c].reshape(rows, width), down[...], (((1,), (1,)), ((), ())), preferred_element_type=F32
        )
        product = jnp.where(mine, product, 0.0)
        folded = product[:, :128]
        for a in range(1, lanes // 128):
            folded = folded + product[:, a * 128:(a + 1) * 128]
        folded = folded + pltpu.roll(folded, rank, 1)
        part[c, 0] = jnp.where(left, folded[:half], folded[half:])
        for j in range(1, shards):
            sends.append(pltpu.make_async_remote_copy(
                src_ref=part.at[c, 0], dst_ref=part.at[c, shards - j],
                send_sem=part_send.at[c, j], recv_sem=part_recv.at[c, shards - j],
                device_id=mate(j), device_id_type=MESH))
            sends[-1].start()
        for j in range(1, shards):
            arrived(part.at[c, j], part_recv.at[c, j], j, mate(j))
        total = part[c, 0]
        for j in range(1, shards):
            total = total + part[c, j]
        turned = pltpu.roll(total, rank, 1)
        low = jnp.concatenate([jnp.where(left, total, turned), jnp.where(left, turned, total)], axis=0)
        spread = jnp.where(mine, jnp.concatenate([low] * (lanes // 128), axis=1), 0.0).astype(BF16)
        if c == 0:
            loads[2].wait()
        for g in range(heads):
            update = jnp.dot(
                spread, up[:, g * span:(g + 1) * span], preferred_element_type=F32
            ).astype(BF16)
            ret[g, c, 0] = update[:TILE]
            delta[g, c] = update.reshape(owners, TILE, span)
            for j in order:
                sends.append(pltpu.make_async_remote_copy(
                    src_ref=delta.at[g, c, j], dst_ref=ret.at[g, c, owners - j],
                    send_sem=ret_send.at[g, c, j], recv_sem=ret_recv.at[g, c, owners - j],
                    device_id=peer(j), device_id_type=MESH))
                sends[-1].start()

    scale = head ** (-0.5)
    spots = chunks * rows
    undo = (iota((requests, spots), 1).astype(F32) == spot).astype(F32).astype(BF16)
    length = to_column(length_ref[...].astype(F32), requests)
    deep = BLOCK * group
    wide = BLOCK * slots
    first = (iota((deep, 1), 0) % BLOCK) * slots
    where_slot = iota((deep, wide), 1)
    for load in loads[3:6]:
        load.wait()
    for g in range(heads):
        loads[6 + 2 * g].wait()
        loads[7 + 2 * g].wait()
        for c in range(chunks):
            for j in range(1, owners):
                arrived(ret.at[g, c, j], ret_recv.at[g, c, j], j, peer(j))
        correction = jnp.dot(undo, ret[g].reshape(spots, span), preferred_element_type=F32)
        query = (base[:, g * span:(g + 1) * span].astype(F32) + correction).astype(BF16).astype(F32)
        fresh_key = tk[:, g * head:(g + 1) * head].astype(F32)
        fresh_value = tv[:, g * head:(g + 1) * head].astype(F32)
        for pair in range(0, requests, 2 * BLOCK):
            outs = []
            for r in (pair, pair + BLOCK):
                here = slice(r, r + BLOCK)
                q = jnp.concatenate([query[here, h * head:(h + 1) * head] for h in range(group)], axis=0)
                keys = kbuf[g, here].reshape(wide, head)
                values = vbuf[g, here].reshape(wide, head)
                scores = lax.dot_general(
                    q.astype(BF16), keys, (((1,), (1,)), ((), ())), preferred_element_type=F32
                ) * scale
                last = first + jnp.concatenate([length[here]] * group, axis=0).astype(jnp.int32)
                valid = (where_slot >= first) & (where_slot < last)
                scores = jnp.where(valid, scores, -1e30)
                fresh = jnp.sum(
                    q * jnp.concatenate([fresh_key[here]] * group, axis=0), axis=1, keepdims=True
                ) * scale
                top = jnp.maximum(jnp.max(scores, axis=1, keepdims=True), fresh)
                expo = jnp.exp(scores - top)
                expo_new = jnp.exp(fresh - top)
                total = jnp.sum(expo, axis=1, keepdims=True) + expo_new
                weights = (expo / total).astype(BF16)
                weight_new = (expo_new / total).astype(BF16).astype(F32)
                mixed = jnp.dot(weights, values, preferred_element_type=F32)
                outs.append(mixed + weight_new * jnp.concatenate([fresh_value[here]] * group, axis=0))
            for h in range(group):
                piece = slice(h * BLOCK, (h + 1) * BLOCK)
                out_ref[pair:pair + 2 * BLOCK, g * span + h * head:g * span + (h + 1) * head] = (
                    jnp.concatenate([out[piece] for out in outs], axis=0).astype(BF16)
                )
    for send in sends:
        send.wait_send()


def body(owners, shards, x, base, tk, tv, k, v, lengths, adapter, storage, down, up):
    requests, width = x.shape
    heads, slots, head = k.shape[1:]
    kept, _, rank = down.shape
    capacity = max(2, 2 * requests // owners)
    chunks = -(-capacity // TILE)
    span = width // heads
    lanes = kept * rank
    down = jnp.swapaxes(down, 1, 2).reshape(lanes, width)
    up = up.reshape(lanes, width)
    small = pl.BlockSpec(memory_space=pltpu.VMEM)
    large = pl.BlockSpec(memory_space=pl.ANY)
    dma = pltpu.SemaphoreType.DMA
    return pl.pallas_call(
        functools.partial(kernel, owners, shards, chunks),
        out_shape=jax.ShapeDtypeStruct((requests, width), BF16),
        in_specs=[small] * 3 + [large] * 8,
        out_specs=pl.BlockSpec(memory_space=pltpu.VMEM),
        scratch_shapes=[
            pltpu.VMEM(x.shape, BF16),
            pltpu.VMEM(base.shape, BF16),
            pltpu.VMEM(tk.shape, BF16),
            pltpu.VMEM(tv.shape, BF16),
            pltpu.VMEM((heads, requests, slots, head), BF16),
            pltpu.VMEM((heads, requests, slots, head), BF16),
            pltpu.VMEM((lanes, width), BF16),
            pltpu.VMEM((lanes, width), BF16),
            pltpu.VMEM((chunks, owners, TILE, width), BF16),
            pltpu.VMEM((chunks, owners, TILE, width), BF16),
            pltpu.VMEM((owners, 8, 128), F32),
            pltpu.VMEM((owners, 8, 128), F32),
            pltpu.VMEM((chunks, shards, owners * TILE // 2, 128), F32),
            pltpu.VMEM((heads, chunks, owners, TILE, span), BF16),
            pltpu.VMEM((heads, chunks, owners, TILE, span), BF16),
            dma((6 + 2 * heads,)),
            dma((chunks, owners)),
            dma((chunks, owners)),
            dma((owners,)),
            dma((owners,)),
            dma((chunks, shards)),
            dma((chunks, shards)),
            dma((heads, chunks, owners)),
            dma((heads, chunks, owners)),
        ],
        compiler_params=pltpu.CompilerParams(
            collective_id=0, has_side_effects=True, vmem_limit_bytes=40 * 1024 * 1024
        ),
    )(
        adapter.reshape(1, requests), storage.reshape(1, -1), lengths.reshape(1, requests),
        x, base, tk, tv, k, v, down, up,
    )


def solution(mesh):
    rows = P(("groups", "inst"), "tp")
    cache = P(("groups", "inst"), "tp", None, None)
    in_specs = (
        rows, rows, rows, rows, cache, cache,
        P(("groups", "inst")),
        P(("groups", "inst")),
        P("groups"),
        P(("groups", "inst"), "tp", None),
        P(("groups", "inst"), None, "tp"),
    )
    step = functools.partial(body, mesh.shape["inst"], mesh.shape["tp"])
    return jax.shard_map(step, mesh=mesh, in_specs=in_specs, out_specs=rows, check_vma=False)
```

```python
import functools

import jax
import jax.numpy as jnp
from jax import lax
from jax.experimental import pallas as pl
from jax.experimental.pallas import tpu as pltpu
from jax.sharding import PartitionSpec as P

MESH = pl.DeviceIdType.MESH
F32 = jnp.float32
BF16 = jnp.bfloat16
TILE = 16
BLOCK = 8


def iota(shape, axis):
    return lax.broadcasted_iota(jnp.int32, shape, axis)


def to_column(row, count):
    shape = (count, row.shape[1])
    return jnp.sum(jnp.where(iota(shape, 0) == iota(shape, 1), row, 0.0), axis=1, keepdims=True)


def to_row(column):
    n = column.shape[0]
    return jnp.sum(jnp.where(iota((n, n), 0) == iota((n, n), 1), column, 0.0), axis=0, keepdims=True)


def kernel(
    owners, shards, chunks,
    adapter_hbm, storage_hbm, length_hbm,
    x_hbm, base_hbm, tk_hbm, tv_hbm, k_hbm, v_hbm, down_hbm, up_hbm,
    out_ref,
    adapter_ref, storage_ref, length_ref, x, base, tk, tv, kbuf, vbuf, down, up,
    snd, arr, tag_snd, tag_arr, part, delta, ret,
    index_sem, in_sem, snd_send, snd_recv, tag_send, tag_recv, part_send, part_recv, ret_send, ret_recv,
):
    me = lax.axis_index("inst")
    tp = lax.axis_index("tp")
    requests, width = x.shape
    heads = kbuf.shape[0]
    slots, head = kbuf.shape[2], kbuf.shape[3]
    span = width // heads
    group = span // head
    lanes = down.shape[0]
    rank = 64
    kept = lanes // rank
    rows = owners * TILE
    peer = lambda j: {"inst": lax.rem(me + j, owners)}
    mate = lambda j: {"tp": lax.rem(tp + j, shards)}

    index_loads = [
        pltpu.make_async_copy(adapter_hbm, adapter_ref, index_sem.at[0]),
        pltpu.make_async_copy(storage_hbm, storage_ref, index_sem.at[1]),
        pltpu.make_async_copy(length_hbm, length_ref, index_sem.at[2]),
    ]
    for load in index_loads:
        load.start()
    loads = [pltpu.make_async_copy(x_hbm, x, in_sem.at[0])]
    loads.append(pltpu.make_async_copy(down_hbm, down, in_sem.at[1]))
    loads.append(pltpu.make_async_copy(up_hbm, up, in_sem.at[2]))
    loads.append(pltpu.make_async_copy(base_hbm, base, in_sem.at[3]))
    loads.append(pltpu.make_async_copy(tk_hbm, tk, in_sem.at[4]))
    loads.append(pltpu.make_async_copy(tv_hbm, tv, in_sem.at[5]))
    for g in range(heads):
        loads.append(pltpu.make_async_copy(k_hbm.at[:, g], kbuf.at[g], in_sem.at[6 + 2 * g]))
        loads.append(pltpu.make_async_copy(v_hbm.at[:, g], vbuf.at[g], in_sem.at[7 + 2 * g]))
    for load in loads:
        load.start()

    barrier = pltpu.get_barrier_semaphore()
    for j in range(1, owners):
        pl.semaphore_signal(barrier, inc=1, device_id=peer(j), device_id_type=MESH)
    for j in range(1, shards):
        pl.semaphore_signal(barrier, inc=1, device_id=mate(j), device_id_type=MESH)

    catalog = storage_ref.shape[1]
    for load in index_loads:
        load.wait()
    adapter = to_column(adapter_ref[...].astype(F32), requests)
    stored = storage_ref[...].astype(F32)
    slot = jnp.sum(
        jnp.where(adapter == iota((requests, catalog), 1).astype(F32), stored, 0.0), axis=1, keepdims=True
    )
    home = jnp.floor((slot + 0.5) * (1.0 / kept))
    tag = slot - home * kept + 1.0
    home = home - me.astype(F32)
    home = jnp.where(home < 0.0, home + owners, home)
    home_row = to_row(home)
    square = (requests, requests)
    earlier = (home == home_row) & (iota(square, 1) < iota(square, 0))
    place = jnp.sum(jnp.where(earlier, 1.0, 0.0), axis=1, keepdims=True)
    turn = jnp.floor((place + 0.5) * (1.0 / TILE))
    spot = turn * rows + home * TILE + (place - turn * TILE)
    spot_row = to_row(spot)

    for j in range(owners):
        shape = (requests, 128)
        here = (home == float(j)) & (place == iota(shape, 1).astype(F32))
        line = jnp.sum(jnp.where(here, tag, 0.0), axis=0, keepdims=True)
        if j:
            tag_snd[j] = jnp.broadcast_to(line, (8, 128))
        else:
            tag_arr[0] = jnp.broadcast_to(line, (8, 128))

    loads[0].wait()
    own = []
    order = sorted(range(1, owners), key=lambda j: (abs(2 * j - owners), j))
    sends, row_sends = [], []
    for c in range(chunks):
        placing = (iota((rows, requests), 0).astype(F32) + float(c * rows) == spot_row)
        packed = jnp.dot(placing.astype(F32).astype(BF16), x[...], preferred_element_type=F32).astype(BF16)
        arr[c, 0] = packed[:TILE]
        snd[c] = packed.reshape(owners, TILE, width)
        if c == 0:
            pl.semaphore_wait(barrier, owners - 1 + shards - 1)
            for j in order:
                sends.append(pltpu.make_async_remote_copy(
                    src_ref=tag_snd.at[j], dst_ref=tag_arr.at[owners - j],
                    send_sem=tag_send.at[j], recv_sem=tag_recv.at[owners - j],
                    device_id=peer(j), device_id_type=MESH))
                sends[-1].start()
        for send in row_sends:
            send.wait_send()
        row_sends = []
        for j in order:
            row_sends.append(pltpu.make_async_remote_copy(
                src_ref=snd.at[c, j], dst_ref=arr.at[c, owners - j],
                send_sem=snd_send.at[c, j], recv_sem=snd_recv.at[c, owners - j],
                device_id=peer(j), device_id_type=MESH))
            row_sends[-1].start()

    sends += row_sends

    def arrived(dst, sem, j, device):
        pltpu.make_async_remote_copy(
            src_ref=dst, dst_ref=dst, send_sem=sem, recv_sem=sem,
            device_id=device, device_id_type=MESH).wait_recv()

    half = rows // 2
    which = iota((rows, lanes), 1) // rank
    left = iota((half, 128), 1) < rank
    tags, back_sends = [], []
    for c in range(chunks):
        if c == 0:
            for j in range(1, owners):
                arrived(tag_arr.at[j], tag_recv.at[j], j, peer(j))
            loads[1].wait()
        columns = []
        for j in range(owners):
            shape = (TILE, 128)
            match = iota(shape, 1) == iota(shape, 0) + c * TILE
            columns.append(jnp.sum(jnp.where(match, tag_arr[j, 0:1, :], 0.0), axis=1, keepdims=True))
        mine = which.astype(F32) == jnp.concatenate(columns, axis=0) - 1.0
        tags.append(mine)
        for j in range(1, owners):
            arrived(arr.at[c, j], snd_recv.at[c, j], j, peer(j))
        product = lax.dot_general(
            arr[c].reshape(rows, width), down[...], (((1,), (1,)), ((), ())), preferred_element_type=F32
        )
        product = jnp.where(mine, product, 0.0)
        folded = product[:, :128]
        for a in range(1, lanes // 128):
            folded = folded + product[:, a * 128:(a + 1) * 128]
        folded = folded + pltpu.roll(folded, rank, 1)
        part[c, 0] = jnp.where(left, folded[:half], folded[half:])
        for j in range(1, shards):
            sends.append(pltpu.make_async_remote_copy(
                src_ref=part.at[c, 0], dst_ref=part.at[c, shards - j],
                send_sem=part_send.at[c, j], recv_sem=part_recv.at[c, shards - j],
                device_id=mate(j), device_id_type=MESH))
            sends[-1].start()
        for j in range(1, shards):
            arrived(part.at[c, j], part_recv.at[c, j], j, mate(j))
        total = part[c, 0]
        for j in range(1, shards):
            total = total + part[c, j]
        turned = pltpu.roll(total, rank, 1)
        low = jnp.concatenate([jnp.where(left, total, turned), jnp.where(left, turned, total)], axis=0)
        spread = jnp.where(mine, jnp.concatenate([low] * (lanes // 128), axis=1), 0.0).astype(BF16)
        if c == 0:
            loads[2].wait()
        for g in range(heads):
            update = jnp.dot(
                spread, up[:, g * span:(g + 1) * span], preferred_element_type=F32
            ).astype(BF16)
            ret[g, c, 0] = update[:TILE]
            delta[g, c] = update.reshape(owners, TILE, span)
            if c == chunks - 1 and g:
                for send in back_sends:
                    send.wait_send()
                back_sends = []
            for j in order:
                back_sends.append(pltpu.make_async_remote_copy(
                    src_ref=delta.at[g, c, j], dst_ref=ret.at[g, c, owners - j],
                    send_sem=ret_send.at[g, c, j], recv_sem=ret_recv.at[g, c, owners - j],
                    device_id=peer(j), device_id_type=MESH))
                back_sends[-1].start()

    scale = head ** (-0.5)
    spots = chunks * rows
    undo = (iota((requests, spots), 1).astype(F32) == spot).astype(F32).astype(BF16)
    length = to_column(length_ref[...].astype(F32), requests)
    deep = BLOCK * group
    wide = BLOCK * slots
    request = iota((deep, 1), 0) % BLOCK
    beside = max(1, 128 // slots)
    lane_tile = beside * slots
    first = (request % beside) * slots
    where_slot = iota((deep, lane_tile), 1)
    holds = [request // beside == t for t in range(wide // lane_tile)]
    for load in loads[3:6]:
        load.wait()
    for g in range(heads):
        loads[6 + 2 * g].wait()
        loads[7 + 2 * g].wait()
        for c in range(chunks):
            for j in range(1, owners):
                arrived(ret.at[g, c, j], ret_recv.at[g, c, j], j, peer(j))
        correction = jnp.dot(undo, ret[g].reshape(spots, span), preferred_element_type=F32)
        query = (base[:, g * span:(g + 1) * span].astype(F32) + correction).astype(BF16).astype(F32)
        fresh_key = tk[:, g * head:(g + 1) * head].astype(F32)
        fresh_value = tv[:, g * head:(g + 1) * head].astype(F32)
        for pair in range(0, requests, 2 * BLOCK):
            outs = []
            for r in (pair, pair + BLOCK):
                here = slice(r, r + BLOCK)
                q = jnp.concatenate([query[here, h * head:(h + 1) * head] for h in range(group)], axis=0)
                keys = kbuf[g, here].reshape(wide, head)
                values = vbuf[g, here].reshape(wide, head)
                scores = lax.dot_general(
                    q.astype(BF16), keys, (((1,), (1,)), ((), ())), preferred_element_type=F32
                )
                last = first + jnp.concatenate([length[here]] * group, axis=0).astype(jnp.int32)
                every, scores = scores, scores[:, :lane_tile]
                for t in range(1, wide // lane_tile):
                    scores = jnp.where(holds[t], every[:, t * lane_tile:(t + 1) * lane_tile], scores)
                valid = (where_slot >= first) & (where_slot < last)
                scores = jnp.where(valid, scores * scale, -1e30)
                fresh = jnp.sum(
                    q * jnp.concatenate([fresh_key[here]] * group, axis=0), axis=1, keepdims=True
                ) * scale
                top = jnp.maximum(jnp.max(scores, axis=1, keepdims=True), fresh)
                expo = jnp.exp(scores - top)
                expo_new = jnp.exp(fresh - top)
                total = jnp.sum(expo, axis=1, keepdims=True) + expo_new
                weights = expo / total
                weights = jnp.concatenate([jnp.where(hold, weights, 0.0) for hold in holds], axis=1).astype(BF16)
                weight_new = (expo_new / total).astype(BF16).astype(F32)
                mixed = jnp.dot(weights, values, preferred_element_type=F32)
                outs.append(mixed + weight_new * jnp.concatenate([fresh_value[here]] * group, axis=0))
            for h in range(group):
                piece = slice(h * BLOCK, (h + 1) * BLOCK)
                out_ref[pair:pair + 2 * BLOCK, g * span + h * head:g * span + (h + 1) * head] = (
                    jnp.concatenate([out[piece] for out in outs], axis=0).astype(BF16)
                )
    for send in sends + back_sends:
        send.wait_send()


def body(owners, shards, x, base, tk, tv, k, v, lengths, adapter, storage, down, up):
    requests, width = x.shape
    heads, slots, head = k.shape[1:]
    kept, _, rank = down.shape
    capacity = max(2, 2 * requests // owners)
    chunks = -(-capacity // TILE)
    span = width // heads
    lanes = kept * rank
    down = jnp.swapaxes(down, 1, 2).reshape(lanes, width)
    up = up.reshape(lanes, width)
    large = pl.BlockSpec(memory_space=pltpu.HBM)
    dma = pltpu.SemaphoreType.DMA
    return pl.pallas_call(
        functools.partial(kernel, owners, shards, chunks),
        out_shape=jax.ShapeDtypeStruct((requests, width), BF16),
        in_specs=[large] * 11,
        out_specs=pl.BlockSpec(memory_space=pltpu.VMEM),
        scratch_shapes=[
            pltpu.VMEM((1, requests), jnp.int32),
            pltpu.VMEM((1, storage.shape[0]), jnp.int32),
            pltpu.VMEM((1, requests), jnp.int32),
            pltpu.VMEM(x.shape, BF16),
            pltpu.VMEM(base.shape, BF16),
            pltpu.VMEM(tk.shape, BF16),
            pltpu.VMEM(tv.shape, BF16),
            pltpu.VMEM((heads, requests, slots, head), BF16),
            pltpu.VMEM((heads, requests, slots, head), BF16),
            pltpu.VMEM((lanes, width), BF16),
            pltpu.VMEM((lanes, width), BF16),
            pltpu.VMEM((chunks, owners, TILE, width), BF16),
            pltpu.VMEM((chunks, owners, TILE, width), BF16),
            pltpu.VMEM((owners, 8, 128), F32),
            pltpu.VMEM((owners, 8, 128), F32),
            pltpu.VMEM((chunks, shards, owners * TILE // 2, 128), F32),
            pltpu.VMEM((heads, chunks, owners, TILE, span), BF16),
            pltpu.VMEM((heads, chunks, owners, TILE, span), BF16),
            dma((3,)),
            dma((6 + 2 * heads,)),
            dma((chunks, owners)),
            dma((chunks, owners)),
            dma((owners,)),
            dma((owners,)),
            dma((chunks, shards)),
            dma((chunks, shards)),
            dma((heads, chunks, owners)),
            dma((heads, chunks, owners)),
        ],
        compiler_params=pltpu.CompilerParams(
            collective_id=0, has_side_effects=True, vmem_limit_bytes=64 * 1024 * 1024
        ),
    )(
        adapter.reshape(1, requests), storage.reshape(1, -1), lengths.reshape(1, requests),
        x, base, tk, tv, k, v, down, up,
    )


def solution(mesh):
    rows = P(("groups", "inst"), "tp")
    cache = P(("groups", "inst"), "tp", None, None)
    in_specs = (
        rows, rows, rows, rows, cache, cache,
        P(("groups", "inst")),
        P(("groups", "inst")),
        P("groups"),
        P(("groups", "inst"), "tp", None),
        P(("groups", "inst"), None, "tp"),
    )
    step = functools.partial(body, mesh.shape["inst"], mesh.shape["tp"])
    return jax.shard_map(step, mesh=mesh, in_specs=in_specs, out_specs=rows, check_vma=False)
```

```python
import functools

import jax
import jax.numpy as jnp
from jax import lax
from jax.experimental import pallas as pl
from jax.experimental.pallas import tpu as pltpu
from jax.sharding import PartitionSpec as P

MESH = pl.DeviceIdType.MESH
F32 = jnp.float32
BF16 = jnp.bfloat16
TILE = 16
BLOCK = 8


def iota(shape, axis):
    return lax.broadcasted_iota(jnp.int32, shape, axis)


def to_column(row, count):
    shape = (count, row.shape[1])
    return jnp.sum(jnp.where(iota(shape, 0) == iota(shape, 1), row, 0.0), axis=1, keepdims=True)


def to_row(column):
    n = column.shape[0]
    return jnp.sum(jnp.where(iota((n, n), 0) == iota((n, n), 1), column, 0.0), axis=0, keepdims=True)


def kernel(
    owners, shards, chunks,
    adapter_hbm, storage_hbm, length_hbm,
    x_hbm, base_hbm, tk_hbm, tv_hbm, k_hbm, v_hbm, down_hbm, up_hbm,
    out_ref,
    adapter_ref, storage_ref, length_ref, x, base, tk, tv, kbuf, vbuf, down, up,
    snd, arr, tag_snd, tag_arr, part, delta, ret,
    index_sem, in_sem, snd_send, snd_recv, tag_send, tag_recv, part_send, part_recv, ret_send, ret_recv,
):
    me = lax.axis_index("inst")
    tp = lax.axis_index("tp")
    requests, width = x.shape
    heads = kbuf.shape[0]
    slots, head = kbuf.shape[2], kbuf.shape[3]
    span = width // heads
    group = span // head
    lanes = down.shape[0]
    rank = 64
    kept = lanes // rank
    rows = owners * TILE
    peer = lambda j: {"inst": lax.rem(me + j, owners)}
    mate = lambda j: {"tp": lax.rem(tp + j, shards)}

    index_loads = [
        pltpu.make_async_copy(adapter_hbm, adapter_ref, index_sem.at[0]),
        pltpu.make_async_copy(storage_hbm, storage_ref, index_sem.at[1]),
        pltpu.make_async_copy(length_hbm, length_ref, index_sem.at[2]),
    ]
    for load in index_loads:
        load.start()
    loads = [pltpu.make_async_copy(x_hbm, x, in_sem.at[0])]
    loads.append(pltpu.make_async_copy(down_hbm, down, in_sem.at[1]))
    loads.append(pltpu.make_async_copy(up_hbm, up, in_sem.at[2]))
    loads.append(pltpu.make_async_copy(base_hbm, base, in_sem.at[3]))
    loads.append(pltpu.make_async_copy(tk_hbm, tk, in_sem.at[4]))
    loads.append(pltpu.make_async_copy(tv_hbm, tv, in_sem.at[5]))
    for g in range(heads):
        loads.append(pltpu.make_async_copy(k_hbm.at[:, g], kbuf.at[g], in_sem.at[6 + 2 * g]))
        loads.append(pltpu.make_async_copy(v_hbm.at[:, g], vbuf.at[g], in_sem.at[7 + 2 * g]))
    for load in loads:
        load.start()

    barrier = pltpu.get_barrier_semaphore()
    for j in range(1, owners):
        pl.semaphore_signal(barrier, inc=1, device_id=peer(j), device_id_type=MESH)
    for j in range(1, shards):
        pl.semaphore_signal(barrier, inc=1, device_id=mate(j), device_id_type=MESH)

    catalog = storage_ref.shape[1]
    for load in index_loads:
        load.wait()
    adapter = to_column(adapter_ref[...].astype(F32), requests)
    stored = storage_ref[...].astype(F32)
    slot = jnp.sum(
        jnp.where(adapter == iota((requests, catalog), 1).astype(F32), stored, 0.0), axis=1, keepdims=True
    )
    home = jnp.floor((slot + 0.5) * (1.0 / kept))
    tag = slot - home * kept + 1.0
    home = home - me.astype(F32)
    home = jnp.where(home < 0.0, home + owners, home)
    home_row = to_row(home)
    square = (requests, requests)
    earlier = (home == home_row) & (iota(square, 1) < iota(square, 0))
    place = jnp.sum(jnp.where(earlier, 1.0, 0.0), axis=1, keepdims=True)
    turn = jnp.floor((place + 0.5) * (1.0 / TILE))
    spot = turn * rows + home * TILE + (place - turn * TILE)
    spot_row = to_row(spot)

    for j in range(owners):
        shape = (requests, 128)
        here = (home == float(j)) & (place == iota(shape, 1).astype(F32))
        line = jnp.sum(jnp.where(here, tag, 0.0), axis=0, keepdims=True)
        if j:
            tag_snd[j] = jnp.broadcast_to(line, (8, 128))
        else:
            tag_arr[0] = jnp.broadcast_to(line, (8, 128))

    loads[0].wait()
    own = []
    order = sorted(range(1, owners), key=lambda j: (abs(2 * j - owners), j))
    sends, row_sends = [], []
    for c in range(chunks):
        placing = (iota((rows, requests), 0).astype(F32) + float(c * rows) == spot_row)
        packed = jnp.dot(placing.astype(F32).astype(BF16), x[...], preferred_element_type=F32).astype(BF16)
        arr[c, 0] = packed[:TILE]
        snd[c] = packed.reshape(owners, TILE, width)
        if c == 0:
            pl.semaphore_wait(barrier, owners - 1 + shards - 1)
            for j in order:
                sends.append(pltpu.make_async_remote_copy(
                    src_ref=tag_snd.at[j], dst_ref=tag_arr.at[owners - j],
                    send_sem=tag_send.at[j], recv_sem=tag_recv.at[owners - j],
                    device_id=peer(j), device_id_type=MESH))
                sends[-1].start()
        for send in row_sends:
            send.wait_send()
        row_sends = []
        for j in order:
            row_sends.append(pltpu.make_async_remote_copy(
                src_ref=snd.at[c, j], dst_ref=arr.at[c, owners - j],
                send_sem=snd_send.at[c, j], recv_sem=snd_recv.at[c, owners - j],
                device_id=peer(j), device_id_type=MESH))
            row_sends[-1].start()

    sends += row_sends

    def arrived(dst, sem, j, device):
        pltpu.make_async_remote_copy(
            src_ref=dst, dst_ref=dst, send_sem=sem, recv_sem=sem,
            device_id=device, device_id_type=MESH).wait_recv()

    half = rows // 2
    which = iota((rows, lanes), 1) // rank
    left = iota((half, 128), 1) < rank
    tags, back_sends = [], []
    for c in range(chunks):
        if c == 0:
            for j in range(1, owners):
                arrived(tag_arr.at[j], tag_recv.at[j], j, peer(j))
            loads[1].wait()
        columns = []
        for j in range(owners):
            shape = (TILE, 128)
            match = iota(shape, 1) == iota(shape, 0) + c * TILE
            columns.append(jnp.sum(jnp.where(match, tag_arr[j, 0:1, :], 0.0), axis=1, keepdims=True))
        mine = which.astype(F32) == jnp.concatenate(columns, axis=0) - 1.0
        tags.append(mine)
        for j in range(1, owners):
            arrived(arr.at[c, j], snd_recv.at[c, j], j, peer(j))
        product = lax.dot_general(
            arr[c].reshape(rows, width), down[...], (((1,), (1,)), ((), ())), preferred_element_type=F32
        )
        product = jnp.where(mine, product, 0.0)
        folded = product[:, :128]
        for a in range(1, lanes // 128):
            folded = folded + product[:, a * 128:(a + 1) * 128]
        folded = folded + pltpu.roll(folded, rank, 1)
        part[c, 0] = jnp.where(left, folded[:half], folded[half:])
        for j in range(1, shards):
            sends.append(pltpu.make_async_remote_copy(
                src_ref=part.at[c, 0], dst_ref=part.at[c, shards - j],
                send_sem=part_send.at[c, j], recv_sem=part_recv.at[c, shards - j],
                device_id=mate(j), device_id_type=MESH))
            sends[-1].start()
        for j in range(1, shards):
            arrived(part.at[c, j], part_recv.at[c, j], j, mate(j))
        total = part[c, 0]
        for j in range(1, shards):
            total = total + part[c, j]
        turned = pltpu.roll(total, rank, 1)
        low = jnp.concatenate([jnp.where(left, total, turned), jnp.where(left, turned, total)], axis=0)
        spread = jnp.where(mine, jnp.concatenate([low] * (lanes // 128), axis=1), 0.0).astype(BF16)
        if c == 0:
            loads[2].wait()
        for g in range(heads):
            update = jnp.dot(
                spread, up[:, g * span:(g + 1) * span], preferred_element_type=F32
            ).astype(BF16)
            ret[g, c, 0] = update[:TILE]
            delta[g, c] = update.reshape(owners, TILE, span)
            if c == chunks - 1 and g:
                for send in back_sends:
                    send.wait_send()
                back_sends = []
            for j in order:
                back_sends.append(pltpu.make_async_remote_copy(
                    src_ref=delta.at[g, c, j], dst_ref=ret.at[g, c, owners - j],
                    send_sem=ret_send.at[g, c, j], recv_sem=ret_recv.at[g, c, owners - j],
                    device_id=peer(j), device_id_type=MESH))
                back_sends[-1].start()

    scale = head ** (-0.5)
    spots = chunks * rows
    undo = (iota((requests, spots), 1).astype(F32) == spot).astype(F32).astype(BF16)
    length = to_column(length_ref[...].astype(F32), requests)
    deep = BLOCK * group
    wide = BLOCK * slots
    request = iota((deep, 1), 0) % BLOCK
    beside = max(1, 128 // slots)
    lane_tile = beside * slots
    holds = [request // beside == t for t in range(wide // lane_tile)]
    upper = request >= BLOCK // 2
    blocks = range(0, requests, BLOCK)

    def in_rows(values):
        return jnp.concatenate([values[r:r + BLOCK] for r in blocks for _ in range(group)], axis=0)

    def beside_halves(cache, g, r):
        middle = r + BLOCK // 2
        return jnp.concatenate(
            [cache[g, r:middle].reshape(-1, head), cache[g, middle:middle + BLOCK // 2].reshape(-1, head)], axis=1
        )

    first = (iota((requests * group, 1), 0) % beside) * slots
    last = first + in_rows(length).astype(jnp.int32)
    where_slot = iota((requests * group, lane_tile), 1)
    valid = (where_slot >= first) & (where_slot < last)
    for load in loads[3:6]:
        load.wait()
    for g in range(heads):
        loads[6 + 2 * g].wait()
        loads[7 + 2 * g].wait()
        for c in range(chunks):
            for j in range(1, owners):
                arrived(ret.at[g, c, j], ret_recv.at[g, c, j], j, peer(j))
        correction = jnp.dot(undo, ret[g].reshape(spots, span), preferred_element_type=F32)
        query = (base[:, g * span:(g + 1) * span].astype(F32) + correction).astype(BF16).astype(F32)
        fresh_key = tk[:, g * head:(g + 1) * head].astype(F32)
        fresh_value = tv[:, g * head:(g + 1) * head].astype(F32)
        queries, folded = [], []
        for r in blocks:
            q = jnp.concatenate([query[r:r + BLOCK, h * head:(h + 1) * head] for h in range(group)], axis=0)
            queries.append(q)
            every = lax.dot_general(
                q.astype(BF16), kbuf[g, r:r + BLOCK].reshape(wide, head), (((1,), (1,)), ((), ())),
                preferred_element_type=F32,
            )
            scores = every[:, :lane_tile]
            for t in range(1, len(holds)):
                scores = jnp.where(holds[t], every[:, t * lane_tile:(t + 1) * lane_tile], scores)
            folded.append(scores)
        scores = jnp.where(valid, jnp.concatenate(folded, axis=0) * scale, -1e30)
        fresh = jnp.sum(jnp.concatenate(queries, axis=0) * in_rows(fresh_key), axis=1, keepdims=True) * scale
        top = jnp.maximum(jnp.max(scores, axis=1, keepdims=True), fresh)
        expo = jnp.exp(scores - top)
        expo_new = jnp.exp(fresh - top)
        inverse = 1.0 / (jnp.sum(expo, axis=1, keepdims=True) + expo_new)
        weights = expo * inverse
        added = (expo_new * inverse).astype(BF16).astype(F32) * in_rows(fresh_value)
        outs = []
        for i, r in enumerate(blocks):
            here = slice(i * deep, (i + 1) * deep)
            spread = jnp.concatenate([jnp.where(hold, weights[here], 0.0) for hold in holds], axis=1)
            mixed = jnp.dot(spread.astype(BF16), vbuf[g, r:r + BLOCK].reshape(wide, head), preferred_element_type=F32)
            outs.append(mixed + added[here])
        for i in range(0, len(blocks), 2):
            for h in range(group):
                piece = slice(h * BLOCK, (h + 1) * BLOCK)
                out_ref[blocks[i]:blocks[i] + 2 * BLOCK, g * span + h * head:g * span + (h + 1) * head] = (
                    jnp.concatenate([outs[i][piece], outs[i + 1][piece]], axis=0).astype(BF16)
                )
    for send in sends + back_sends:
        send.wait_send()


def body(owners, shards, x, base, tk, tv, k, v, lengths, adapter, storage, down, up):
    requests, width = x.shape
    heads, slots, head = k.shape[1:]
    kept, _, rank = down.shape
    capacity = max(2, 2 * requests // owners)
    chunks = -(-capacity // TILE)
    span = width // heads
    lanes = kept * rank
    down = jnp.swapaxes(down, 1, 2).reshape(lanes, width)
    up = up.reshape(lanes, width)
    large = pl.BlockSpec(memory_space=pltpu.HBM)
    dma = pltpu.SemaphoreType.DMA
    return pl.pallas_call(
        functools.partial(kernel, owners, shards, chunks),
        out_shape=jax.ShapeDtypeStruct((requests, width), BF16),
        in_specs=[large] * 11,
        out_specs=pl.BlockSpec(memory_space=pltpu.VMEM),
        scratch_shapes=[
            pltpu.VMEM((1, requests), jnp.int32),
            pltpu.VMEM((1, storage.shape[0]), jnp.int32),
            pltpu.VMEM((1, requests), jnp.int32),
            pltpu.VMEM(x.shape, BF16),
            pltpu.VMEM(base.shape, BF16),
            pltpu.VMEM(tk.shape, BF16),
            pltpu.VMEM(tv.shape, BF16),
            pltpu.VMEM((heads, requests, slots, head), BF16),
            pltpu.VMEM((heads, requests, slots, head), BF16),
            pltpu.VMEM((lanes, width), BF16),
            pltpu.VMEM((lanes, width), BF16),
            pltpu.VMEM((chunks, owners, TILE, width), BF16),
            pltpu.VMEM((chunks, owners, TILE, width), BF16),
            pltpu.VMEM((owners, 8, 128), F32),
            pltpu.VMEM((owners, 8, 128), F32),
            pltpu.VMEM((chunks, shards, owners * TILE // 2, 128), F32),
            pltpu.VMEM((heads, chunks, owners, TILE, span), BF16),
            pltpu.VMEM((heads, chunks, owners, TILE, span), BF16),
            dma((3,)),
            dma((6 + 2 * heads,)),
            dma((chunks, owners)),
            dma((chunks, owners)),
            dma((owners,)),
            dma((owners,)),
            dma((chunks, shards)),
            dma((chunks, shards)),
            dma((heads, chunks, owners)),
            dma((heads, chunks, owners)),
        ],
        compiler_params=pltpu.CompilerParams(
            collective_id=0, has_side_effects=True, vmem_limit_bytes=64 * 1024 * 1024
        ),
    )(
        adapter.reshape(1, requests), storage.reshape(1, -1), lengths.reshape(1, requests),
        x, base, tk, tv, k, v, down, up,
    )


def solution(mesh):
    rows = P(("groups", "inst"), "tp")
    cache = P(("groups", "inst"), "tp", None, None)
    in_specs = (
        rows, rows, rows, rows, cache, cache,
        P(("groups", "inst")),
        P(("groups", "inst")),
        P("groups"),
        P(("groups", "inst"), "tp", None),
        P(("groups", "inst"), None, "tp"),
    )
    step = functools.partial(body, mesh.shape["inst"], mesh.shape["tp"])
    return jax.shard_map(step, mesh=mesh, in_specs=in_specs, out_specs=rows, check_vma=False)
```

```python
import functools

import jax
import jax.numpy as jnp
from jax import lax
from jax.experimental import pallas as pl
from jax.experimental.pallas import tpu as pltpu
from jax.sharding import PartitionSpec as P

MESH = pl.DeviceIdType.MESH
F32 = jnp.float32
BF16 = jnp.bfloat16
TILE = 16
BLOCK = 8


def iota(shape, axis):
    return lax.broadcasted_iota(jnp.int32, shape, axis)


def to_column(row, count):
    shape = (count, row.shape[1])
    return jnp.sum(jnp.where(iota(shape, 0) == iota(shape, 1), row, 0.0), axis=1, keepdims=True)


def to_row(column):
    n = column.shape[0]
    return jnp.sum(jnp.where(iota((n, n), 0) == iota((n, n), 1), column, 0.0), axis=0, keepdims=True)


def kernel(
    owners, shards, chunks,
    adapter_hbm, storage_hbm, length_hbm,
    x_hbm, base_hbm, tk_hbm, tv_hbm, k_hbm, v_hbm, down_hbm, up_hbm,
    out_ref,
    adapter_ref, storage_ref, length_ref, x, base, tk, tv, kbuf, vbuf, down, up,
    snd, arr, tag_snd, tag_arr, part, delta, ret,
    index_sem, in_sem, snd_send, snd_recv, tag_send, tag_recv, part_send, part_recv, ret_send, ret_recv,
):
    me = lax.axis_index("inst")
    tp = lax.axis_index("tp")
    requests, width = x.shape
    heads = kbuf.shape[0]
    slots, head = kbuf.shape[2], kbuf.shape[3]
    span = width // heads
    group = span // head
    lanes = down.shape[0]
    rank = 64
    kept = lanes // rank
    rows = owners * TILE
    peer = lambda j: {"inst": lax.rem(me + j, owners)}
    mate = lambda j: {"tp": lax.rem(tp + j, shards)}

    index_loads = [
        pltpu.make_async_copy(adapter_hbm, adapter_ref, index_sem.at[0]),
        pltpu.make_async_copy(storage_hbm, storage_ref, index_sem.at[1]),
        pltpu.make_async_copy(length_hbm, length_ref, index_sem.at[2]),
    ]
    for load in index_loads:
        load.start()
    loads = [pltpu.make_async_copy(x_hbm, x, in_sem.at[0])]
    loads.append(pltpu.make_async_copy(down_hbm, down, in_sem.at[1]))
    loads.append(pltpu.make_async_copy(up_hbm, up, in_sem.at[2]))
    loads.append(pltpu.make_async_copy(base_hbm, base, in_sem.at[3]))
    loads.append(pltpu.make_async_copy(tk_hbm, tk, in_sem.at[4]))
    loads.append(pltpu.make_async_copy(tv_hbm, tv, in_sem.at[5]))
    for g in range(heads):
        loads.append(pltpu.make_async_copy(k_hbm.at[:, g], kbuf.at[g], in_sem.at[6 + 2 * g]))
        loads.append(pltpu.make_async_copy(v_hbm.at[:, g], vbuf.at[g], in_sem.at[7 + 2 * g]))
    for load in loads:
        load.start()

    barrier = pltpu.get_barrier_semaphore()
    for j in range(1, owners):
        pl.semaphore_signal(barrier, inc=1, device_id=peer(j), device_id_type=MESH)
    for j in range(1, shards):
        pl.semaphore_signal(barrier, inc=1, device_id=mate(j), device_id_type=MESH)

    catalog = storage_ref.shape[1]
    for load in index_loads:
        load.wait()
    adapter = to_column(adapter_ref[...].astype(F32), requests)
    stored = storage_ref[...].astype(F32)
    slot = jnp.sum(
        jnp.where(adapter == iota((requests, catalog), 1).astype(F32), stored, 0.0), axis=1, keepdims=True
    )
    home = jnp.floor((slot + 0.5) * (1.0 / kept))
    tag = slot - home * kept + 1.0
    home = home - me.astype(F32)
    home = jnp.where(home < 0.0, home + owners, home)
    home_row = to_row(home)
    square = (requests, requests)
    earlier = (home == home_row) & (iota(square, 1) < iota(square, 0))
    place = jnp.sum(jnp.where(earlier, 1.0, 0.0), axis=1, keepdims=True)
    turn = jnp.floor((place + 0.5) * (1.0 / TILE))
    spot = turn * rows + home * TILE + (place - turn * TILE)
    spot_row = to_row(spot)

    for j in range(owners):
        shape = (requests, 128)
        here = (home == float(j)) & (place == iota(shape, 1).astype(F32))
        line = jnp.sum(jnp.where(here, tag, 0.0), axis=0, keepdims=True)
        if j:
            tag_snd[j] = jnp.broadcast_to(line, (8, 128))
        else:
            tag_arr[0] = jnp.broadcast_to(line, (8, 128))

    loads[0].wait()
    own = []
    order = sorted(range(1, owners), key=lambda j: (abs(2 * j - owners), j))
    sends, row_sends = [], []
    for c in range(chunks):
        placing = (iota((rows, requests), 0).astype(F32) + float(c * rows) == spot_row)
        packed = jnp.dot(placing.astype(F32).astype(BF16), x[...], preferred_element_type=F32).astype(BF16)
        arr[c, 0] = packed[:TILE]
        snd[c] = packed.reshape(owners, TILE, width)
        if c == 0:
            pl.semaphore_wait(barrier, owners - 1 + shards - 1)
            for j in order:
                sends.append(pltpu.make_async_remote_copy(
                    src_ref=tag_snd.at[j], dst_ref=tag_arr.at[owners - j],
                    send_sem=tag_send.at[j], recv_sem=tag_recv.at[owners - j],
                    device_id=peer(j), device_id_type=MESH))
                sends[-1].start()
        ahead, row_sends = row_sends, []
        for i, j in enumerate(order):
            if ahead:
                ahead[i].wait_send()
            row_sends.append(pltpu.make_async_remote_copy(
                src_ref=snd.at[c, j], dst_ref=arr.at[c, owners - j],
                send_sem=snd_send.at[c, j], recv_sem=snd_recv.at[c, owners - j],
                device_id=peer(j), device_id_type=MESH))
            row_sends[-1].start()

    sends += row_sends

    def arrived(dst, sem, j, device):
        pltpu.make_async_remote_copy(
            src_ref=dst, dst_ref=dst, send_sem=sem, recv_sem=sem,
            device_id=device, device_id_type=MESH).wait_recv()

    half = rows // 2
    which = iota((rows, lanes), 1) // rank
    left = iota((half, 128), 1) < rank
    tags, back_sends = [], []
    for c in range(chunks):
        if c == 0:
            for j in range(1, owners):
                arrived(tag_arr.at[j], tag_recv.at[j], j, peer(j))
            loads[1].wait()
        columns = []
        for j in range(owners):
            shape = (TILE, 128)
            match = iota(shape, 1) == iota(shape, 0) + c * TILE
            columns.append(jnp.sum(jnp.where(match, tag_arr[j, 0:1, :], 0.0), axis=1, keepdims=True))
        mine = which.astype(F32) == jnp.concatenate(columns, axis=0) - 1.0
        tags.append(mine)
        for j in range(1, owners):
            arrived(arr.at[c, j], snd_recv.at[c, j], j, peer(j))
        product = lax.dot_general(
            arr[c].reshape(rows, width), down[...], (((1,), (1,)), ((), ())), preferred_element_type=F32
        )
        product = jnp.where(mine, product, 0.0)
        folded = product[:, :128]
        for a in range(1, lanes // 128):
            folded = folded + product[:, a * 128:(a + 1) * 128]
        folded = folded + pltpu.roll(folded, rank, 1)
        part[c, 0] = jnp.where(left, folded[:half], folded[half:])
        for j in range(1, shards):
            sends.append(pltpu.make_async_remote_copy(
                src_ref=part.at[c, 0], dst_ref=part.at[c, shards - j],
                send_sem=part_send.at[c, j], recv_sem=part_recv.at[c, shards - j],
                device_id=mate(j), device_id_type=MESH))
            sends[-1].start()
        for j in range(1, shards):
            arrived(part.at[c, j], part_recv.at[c, j], j, mate(j))
        total = part[c, 0]
        for j in range(1, shards):
            total = total + part[c, j]
        turned = pltpu.roll(total, rank, 1)
        low = jnp.concatenate([jnp.where(left, total, turned), jnp.where(left, turned, total)], axis=0)
        spread = jnp.where(mine, jnp.concatenate([low] * (lanes // 128), axis=1), 0.0).astype(BF16)
        if c == 0:
            loads[2].wait()
        for g in range(heads):
            update = jnp.dot(
                spread, up[:, g * span:(g + 1) * span], preferred_element_type=F32
            ).astype(BF16)
            ret[g, c, 0] = update[:TILE]
            delta[g, c] = update.reshape(owners, TILE, span)
            for j in order:
                back_sends.append(pltpu.make_async_remote_copy(
                    src_ref=delta.at[g, c, j], dst_ref=ret.at[g, c, owners - j],
                    send_sem=ret_send.at[g, c, j], recv_sem=ret_recv.at[g, c, owners - j],
                    device_id=peer(j), device_id_type=MESH))
                back_sends[-1].start()

    scale = head ** (-0.5)
    spots = chunks * rows
    undo = (iota((requests, spots), 1).astype(F32) == spot).astype(F32).astype(BF16)
    length = to_column(length_ref[...].astype(F32), requests)
    deep = BLOCK * group
    wide = BLOCK * slots
    request = iota((deep, 1), 0) % BLOCK
    beside = max(1, 128 // slots)
    lane_tile = beside * slots
    holds = [request // beside == t for t in range(wide // lane_tile)]
    upper = request >= BLOCK // 2
    blocks = range(0, requests, BLOCK)

    def in_rows(values):
        return jnp.concatenate([values[r:r + BLOCK] for r in blocks for _ in range(group)], axis=0)

    def beside_halves(cache, g, r):
        middle = r + BLOCK // 2
        return jnp.concatenate(
            [cache[g, r:middle].reshape(-1, head), cache[g, middle:middle + BLOCK // 2].reshape(-1, head)], axis=1
        )

    first = (iota((requests * group, 1), 0) % beside) * slots
    last = first + in_rows(length).astype(jnp.int32)
    where_slot = iota((requests * group, lane_tile), 1)
    valid = (where_slot >= first) & (where_slot < last)
    for load in loads[3:6]:
        load.wait()
    for g in range(heads):
        loads[6 + 2 * g].wait()
        loads[7 + 2 * g].wait()
        for c in range(chunks):
            for j in range(1, owners):
                arrived(ret.at[g, c, j], ret_recv.at[g, c, j], j, peer(j))
        correction = jnp.dot(undo, ret[g].reshape(spots, span), preferred_element_type=F32)
        query = (base[:, g * span:(g + 1) * span].astype(F32) + correction).astype(BF16).astype(F32)
        fresh_key = tk[:, g * head:(g + 1) * head].astype(F32)
        fresh_value = tv[:, g * head:(g + 1) * head].astype(F32)
        queries, folded = [], []
        for r in blocks:
            q = jnp.concatenate([query[r:r + BLOCK, h * head:(h + 1) * head] for h in range(group)], axis=0)
            queries.append(q)
            every = lax.dot_general(
                q.astype(BF16), kbuf[g, r:r + BLOCK].reshape(wide, head), (((1,), (1,)), ((), ())),
                preferred_element_type=F32,
            )
            scores = every[:, :lane_tile]
            for t in range(1, len(holds)):
                scores = jnp.where(holds[t], every[:, t * lane_tile:(t + 1) * lane_tile], scores)
            folded.append(scores)
        scores = jnp.where(valid, jnp.concatenate(folded, axis=0) * scale, -1e30)
        fresh = jnp.sum(jnp.concatenate(queries, axis=0) * in_rows(fresh_key), axis=1, keepdims=True) * scale
        top = jnp.maximum(jnp.max(scores, axis=1, keepdims=True), fresh)
        expo = jnp.exp(scores - top)
        expo_new = jnp.exp(fresh - top)
        inverse = 1.0 / (jnp.sum(expo, axis=1, keepdims=True) + expo_new)
        weights = expo * inverse
        added = (expo_new * inverse).astype(BF16).astype(F32) * in_rows(fresh_value)
        outs = []
        for i, r in enumerate(blocks):
            here = slice(i * deep, (i + 1) * deep)
            spread = jnp.concatenate([jnp.where(hold, weights[here], 0.0) for hold in holds], axis=1)
            mixed = jnp.dot(spread.astype(BF16), vbuf[g, r:r + BLOCK].reshape(wide, head), preferred_element_type=F32)
            outs.append(mixed + added[here])
        for i in range(0, len(blocks), 2):
            for h in range(group):
                piece = slice(h * BLOCK, (h + 1) * BLOCK)
                out_ref[blocks[i]:blocks[i] + 2 * BLOCK, g * span + h * head:g * span + (h + 1) * head] = (
                    jnp.concatenate([outs[i][piece], outs[i + 1][piece]], axis=0).astype(BF16)
                )
    for send in sends + back_sends:
        send.wait_send()


def body(owners, shards, x, base, tk, tv, k, v, lengths, adapter, storage, down, up):
    requests, width = x.shape
    heads, slots, head = k.shape[1:]
    kept, _, rank = down.shape
    capacity = max(2, 2 * requests // owners)
    chunks = -(-capacity // TILE)
    span = width // heads
    lanes = kept * rank
    down = jnp.swapaxes(down, 1, 2).reshape(lanes, width)
    up = up.reshape(lanes, width)
    large = pl.BlockSpec(memory_space=pltpu.HBM)
    dma = pltpu.SemaphoreType.DMA
    return pl.pallas_call(
        functools.partial(kernel, owners, shards, chunks),
        out_shape=jax.ShapeDtypeStruct((requests, width), BF16),
        in_specs=[large] * 11,
        out_specs=pl.BlockSpec(memory_space=pltpu.VMEM),
        scratch_shapes=[
            pltpu.VMEM((1, requests), jnp.int32),
            pltpu.VMEM((1, storage.shape[0]), jnp.int32),
            pltpu.VMEM((1, requests), jnp.int32),
            pltpu.VMEM(x.shape, BF16),
            pltpu.VMEM(base.shape, BF16),
            pltpu.VMEM(tk.shape, BF16),
            pltpu.VMEM(tv.shape, BF16),
            pltpu.VMEM((heads, requests, slots, head), BF16),
            pltpu.VMEM((heads, requests, slots, head), BF16),
            pltpu.VMEM((lanes, width), BF16),
            pltpu.VMEM((lanes, width), BF16),
            pltpu.VMEM((chunks, owners, TILE, width), BF16),
            pltpu.VMEM((chunks, owners, TILE, width), BF16),
            pltpu.VMEM((owners, 8, 128), F32),
            pltpu.VMEM((owners, 8, 128), F32),
            pltpu.VMEM((chunks, shards, owners * TILE // 2, 128), F32),
            pltpu.VMEM((heads, chunks, owners, TILE, span), BF16),
            pltpu.VMEM((heads, chunks, owners, TILE, span), BF16),
            dma((3,)),
            dma((6 + 2 * heads,)),
            dma((chunks, owners)),
            dma((chunks, owners)),
            dma((owners,)),
            dma((owners,)),
            dma((chunks, shards)),
            dma((chunks, shards)),
            dma((heads, chunks, owners)),
            dma((heads, chunks, owners)),
        ],
        compiler_params=pltpu.CompilerParams(
            collective_id=0, has_side_effects=True, vmem_limit_bytes=64 * 1024 * 1024
        ),
    )(
        adapter.reshape(1, requests), storage.reshape(1, -1), lengths.reshape(1, requests),
        x, base, tk, tv, k, v, down, up,
    )


def solution(mesh):
    rows = P(("groups", "inst"), "tp")
    cache = P(("groups", "inst"), "tp", None, None)
    in_specs = (
        rows, rows, rows, rows, cache, cache,
        P(("groups", "inst")),
        P(("groups", "inst")),
        P("groups"),
        P(("groups", "inst"), "tp", None),
        P(("groups", "inst"), None, "tp"),
    )
    step = functools.partial(body, mesh.shape["inst"], mesh.shape["tp"])
    return jax.shard_map(step, mesh=mesh, in_specs=in_specs, out_specs=rows, check_vma=False)
```

```python
import functools

import jax
import jax.numpy as jnp
from jax import lax
from jax.experimental import pallas as pl
from jax.experimental.pallas import tpu as pltpu
from jax.sharding import PartitionSpec as P

MESH = pl.DeviceIdType.MESH
F32 = jnp.float32
BF16 = jnp.bfloat16
TILE = 16
BLOCK = 8


def iota(shape, axis):
    return lax.broadcasted_iota(jnp.int32, shape, axis)


def to_column(row, count):
    shape = (count, row.shape[1])
    return jnp.sum(jnp.where(iota(shape, 0) == iota(shape, 1), row, 0.0), axis=1, keepdims=True)


def to_row(column):
    n = column.shape[0]
    return jnp.sum(jnp.where(iota((n, n), 0) == iota((n, n), 1), column, 0.0), axis=0, keepdims=True)


def kernel(
    owners, shards, chunks,
    adapter_hbm, storage_hbm, length_hbm,
    x_hbm, base_hbm, tk_hbm, tv_hbm, k_hbm, v_hbm, down_hbm, up_hbm,
    out_ref,
    adapter_ref, storage_ref, length_ref, x, base, tk, tv, kbuf, vbuf, down, up,
    snd, arr, tag_snd, tag_arr, part, delta, ret,
    index_sem, in_sem, snd_send, snd_recv, tag_send, tag_recv, part_send, part_recv, ret_send, ret_recv,
):
    me = lax.axis_index("inst")
    tp = lax.axis_index("tp")
    requests, width = x.shape
    heads = kbuf.shape[0]
    slots, head = kbuf.shape[2], kbuf.shape[3]
    span = width // heads
    group = span // head
    lanes = down.shape[0]
    rank = 64
    kept = lanes // rank
    rows = owners * TILE
    peer = lambda j: {"inst": lax.rem(me + j, owners)}
    mate = lambda j: {"tp": lax.rem(tp + j, shards)}

    index_loads = [
        pltpu.make_async_copy(adapter_hbm, adapter_ref, index_sem.at[0]),
        pltpu.make_async_copy(storage_hbm, storage_ref, index_sem.at[1]),
        pltpu.make_async_copy(length_hbm, length_ref, index_sem.at[2]),
    ]
    for load in index_loads:
        load.start()
    loads = [pltpu.make_async_copy(x_hbm, x, in_sem.at[0])]
    loads.append(pltpu.make_async_copy(down_hbm, down, in_sem.at[1]))
    loads.append(pltpu.make_async_copy(up_hbm, up, in_sem.at[2]))
    loads.append(pltpu.make_async_copy(base_hbm, base, in_sem.at[3]))
    loads.append(pltpu.make_async_copy(tk_hbm, tk, in_sem.at[4]))
    loads.append(pltpu.make_async_copy(tv_hbm, tv, in_sem.at[5]))
    for g in range(heads):
        loads.append(pltpu.make_async_copy(k_hbm.at[:, g], kbuf.at[g], in_sem.at[6 + 2 * g]))
        loads.append(pltpu.make_async_copy(v_hbm.at[:, g], vbuf.at[g], in_sem.at[7 + 2 * g]))
    for load in loads:
        load.start()

    barrier = pltpu.get_barrier_semaphore()
    for j in range(1, owners):
        pl.semaphore_signal(barrier, inc=1, device_id=peer(j), device_id_type=MESH)
    for j in range(1, shards):
        pl.semaphore_signal(barrier, inc=1, device_id=mate(j), device_id_type=MESH)

    catalog = storage_ref.shape[1]
    for load in index_loads:
        load.wait()
    adapter = to_column(adapter_ref[...].astype(F32), requests)
    stored = storage_ref[...].astype(F32)
    slot = jnp.sum(
        jnp.where(adapter == iota((requests, catalog), 1).astype(F32), stored, 0.0), axis=1, keepdims=True
    )
    home = jnp.floor((slot + 0.5) * (1.0 / kept))
    tag = slot - home * kept + 1.0
    home = home - me.astype(F32)
    home = jnp.where(home < 0.0, home + owners, home)
    home_row = to_row(home)
    square = (requests, requests)
    earlier = (home == home_row) & (iota(square, 1) < iota(square, 0))
    place = jnp.sum(jnp.where(earlier, 1.0, 0.0), axis=1, keepdims=True)
    turn = jnp.floor((place + 0.5) * (1.0 / TILE))
    spot = turn * rows + home * TILE + (place - turn * TILE)
    spot_row = to_row(spot)

    for j in range(owners):
        shape = (requests, 128)
        here = (home == float(j)) & (place == iota(shape, 1).astype(F32))
        line = jnp.sum(jnp.where(here, tag, 0.0), axis=0, keepdims=True)
        if j:
            tag_snd[j] = jnp.broadcast_to(line, (8, 128))
        else:
            tag_arr[0] = jnp.broadcast_to(line, (8, 128))

    loads[0].wait()
    own = []
    order = sorted(range(1, owners), key=lambda j: (abs(2 * j - owners), j))
    sends, row_sends = [], []
    for c in range(chunks):
        placing = (iota((rows, requests), 0).astype(F32) + float(c * rows) == spot_row)
        packed = jnp.dot(placing.astype(F32).astype(BF16), x[...], preferred_element_type=F32).astype(BF16)
        arr[c, 0] = packed[:TILE]
        snd[c] = packed.reshape(owners, TILE, width)
        if c == 0:
            pl.semaphore_wait(barrier, owners - 1 + shards - 1)
            for j in order:
                sends.append(pltpu.make_async_remote_copy(
                    src_ref=tag_snd.at[j], dst_ref=tag_arr.at[owners - j],
                    send_sem=tag_send.at[j], recv_sem=tag_recv.at[owners - j],
                    device_id=peer(j), device_id_type=MESH))
                sends[-1].start()
        ahead, row_sends = row_sends, []
        for i, j in enumerate(order):
            if ahead:
                ahead[i].wait_send()
            row_sends.append(pltpu.make_async_remote_copy(
                src_ref=snd.at[c, j], dst_ref=arr.at[c, owners - j],
                send_sem=snd_send.at[c, j], recv_sem=snd_recv.at[c, owners - j],
                device_id=peer(j), device_id_type=MESH))
            row_sends[-1].start()

    sends += row_sends

    def arrived(dst, sem, j, device):
        pltpu.make_async_remote_copy(
            src_ref=dst, dst_ref=dst, send_sem=sem, recv_sem=sem,
            device_id=device, device_id_type=MESH).wait_recv()

    pieces_of = lambda c: heads if c == chunks - 1 else 1
    half = rows // 2
    which = iota((rows, lanes), 1) // rank
    left = iota((half, 128), 1) < rank
    tags, back_sends = [], []
    for c in range(chunks):
        if c == 0:
            for j in range(1, owners):
                arrived(tag_arr.at[j], tag_recv.at[j], j, peer(j))
            loads[1].wait()
        columns = []
        for j in range(owners):
            shape = (TILE, 128)
            match = iota(shape, 1) == iota(shape, 0) + c * TILE
            columns.append(jnp.sum(jnp.where(match, tag_arr[j, 0:1, :], 0.0), axis=1, keepdims=True))
        mine = which.astype(F32) == jnp.concatenate(columns, axis=0) - 1.0
        tags.append(mine)
        for j in range(1, owners):
            arrived(arr.at[c, j], snd_recv.at[c, j], j, peer(j))
        product = lax.dot_general(
            arr[c].reshape(rows, width), down[...], (((1,), (1,)), ((), ())), preferred_element_type=F32
        )
        product = jnp.where(mine, product, 0.0)
        folded = product[:, :128]
        for a in range(1, lanes // 128):
            folded = folded + product[:, a * 128:(a + 1) * 128]
        folded = folded + pltpu.roll(folded, rank, 1)
        part[c, 0] = jnp.where(left, folded[:half], folded[half:])
        for j in range(1, shards):
            sends.append(pltpu.make_async_remote_copy(
                src_ref=part.at[c, 0], dst_ref=part.at[c, shards - j],
                send_sem=part_send.at[c, j], recv_sem=part_recv.at[c, shards - j],
                device_id=mate(j), device_id_type=MESH))
            sends[-1].start()
        for j in range(1, shards):
            arrived(part.at[c, j], part_recv.at[c, j], j, mate(j))
        total = part[c, 0]
        for j in range(1, shards):
            total = total + part[c, j]
        turned = pltpu.roll(total, rank, 1)
        low = jnp.concatenate([jnp.where(left, total, turned), jnp.where(left, turned, total)], axis=0)
        spread = jnp.where(mine, jnp.concatenate([low] * (lanes // 128), axis=1), 0.0).astype(BF16)
        if c == 0:
            loads[2].wait()
        pieces = pieces_of(c)
        columns = width // pieces
        for g in range(pieces):
            across = slice(g * columns, (g + 1) * columns)
            update = jnp.dot(spread, up[:, across], preferred_element_type=F32).astype(BF16)
            ret[c, 0, :, across] = update[:TILE]
            delta[c, :, :, across] = update.reshape(owners, TILE, columns)
            for j in order:
                back_sends.append(pltpu.make_async_remote_copy(
                    src_ref=delta.at[c, j, :, across], dst_ref=ret.at[c, owners - j, :, across],
                    send_sem=ret_send.at[g, c, j], recv_sem=ret_recv.at[g, c, owners - j],
                    device_id=peer(j), device_id_type=MESH))
                back_sends[-1].start()

    scale = head ** (-0.5)
    spots = chunks * rows
    undo = (iota((requests, spots), 1).astype(F32) == spot).astype(F32).astype(BF16)
    length = to_column(length_ref[...].astype(F32), requests)
    deep = BLOCK * group
    wide = BLOCK * slots
    request = iota((deep, 1), 0) % BLOCK
    beside = max(1, 128 // slots)
    lane_tile = beside * slots
    holds = [request // beside == t for t in range(wide // lane_tile)]
    upper = request >= BLOCK // 2
    blocks = range(0, requests, BLOCK)

    def in_rows(values):
        return jnp.concatenate([values[r:r + BLOCK] for r in blocks for _ in range(group)], axis=0)

    def beside_halves(cache, g, r):
        middle = r + BLOCK // 2
        return jnp.concatenate(
            [cache[g, r:middle].reshape(-1, head), cache[g, middle:middle + BLOCK // 2].reshape(-1, head)], axis=1
        )

    first = (iota((requests * group, 1), 0) % beside) * slots
    last = first + in_rows(length).astype(jnp.int32)
    where_slot = iota((requests * group, lane_tile), 1)
    valid = (where_slot >= first) & (where_slot < last)
    for load in loads[3:6]:
        load.wait()
    for g in range(heads):
        loads[6 + 2 * g].wait()
        loads[7 + 2 * g].wait()
        for c in range(chunks):
            pieces = pieces_of(c)
            if g < pieces:
                across = slice(g * (width // pieces), (g + 1) * (width // pieces))
                for j in range(1, owners):
                    arrived(ret.at[c, j, :, across], ret_recv.at[g, c, j], j, peer(j))
        correction = jnp.dot(undo, ret[:, :, :, g * span:(g + 1) * span].reshape(spots, span), preferred_element_type=F32)
        query = (base[:, g * span:(g + 1) * span].astype(F32) + correction).astype(BF16).astype(F32)
        fresh_key = tk[:, g * head:(g + 1) * head].astype(F32)
        fresh_value = tv[:, g * head:(g + 1) * head].astype(F32)
        queries, folded = [], []
        for r in blocks:
            q = jnp.concatenate([query[r:r + BLOCK, h * head:(h + 1) * head] for h in range(group)], axis=0)
            queries.append(q)
            every = lax.dot_general(
                q.astype(BF16), kbuf[g, r:r + BLOCK].reshape(wide, head), (((1,), (1,)), ((), ())),
                preferred_element_type=F32,
            )
            scores = every[:, :lane_tile]
            for t in range(1, len(holds)):
                scores = jnp.where(holds[t], every[:, t * lane_tile:(t + 1) * lane_tile], scores)
            folded.append(scores)
        scores = jnp.where(valid, jnp.concatenate(folded, axis=0) * scale, -1e30)
        fresh = jnp.sum(jnp.concatenate(queries, axis=0) * in_rows(fresh_key), axis=1, keepdims=True) * scale
        top = jnp.maximum(jnp.max(scores, axis=1, keepdims=True), fresh)
        expo = jnp.exp(scores - top)
        expo_new = jnp.exp(fresh - top)
        inverse = 1.0 / (jnp.sum(expo, axis=1, keepdims=True) + expo_new)
        weights = expo * inverse
        added = (expo_new * inverse).astype(BF16).astype(F32) * in_rows(fresh_value)
        outs = []
        for i, r in enumerate(blocks):
            here = slice(i * deep, (i + 1) * deep)
            spread = jnp.concatenate([jnp.where(hold, weights[here], 0.0) for hold in holds], axis=1)
            mixed = jnp.dot(spread.astype(BF16), vbuf[g, r:r + BLOCK].reshape(wide, head), preferred_element_type=F32)
            outs.append(mixed + added[here])
        for i in range(0, len(blocks), 2):
            for h in range(group):
                piece = slice(h * BLOCK, (h + 1) * BLOCK)
                out_ref[blocks[i]:blocks[i] + 2 * BLOCK, g * span + h * head:g * span + (h + 1) * head] = (
                    jnp.concatenate([outs[i][piece], outs[i + 1][piece]], axis=0).astype(BF16)
                )
    for send in sends + back_sends:
        send.wait_send()


def body(owners, shards, x, base, tk, tv, k, v, lengths, adapter, storage, down, up):
    requests, width = x.shape
    heads, slots, head = k.shape[1:]
    kept, _, rank = down.shape
    capacity = max(2, 2 * requests // owners)
    chunks = -(-capacity // TILE)
    span = width // heads
    lanes = kept * rank
    down = jnp.swapaxes(down, 1, 2).reshape(lanes, width)
    up = up.reshape(lanes, width)
    large = pl.BlockSpec(memory_space=pltpu.HBM)
    dma = pltpu.SemaphoreType.DMA
    return pl.pallas_call(
        functools.partial(kernel, owners, shards, chunks),
        out_shape=jax.ShapeDtypeStruct((requests, width), BF16),
        in_specs=[large] * 11,
        out_specs=pl.BlockSpec(memory_space=pltpu.VMEM),
        scratch_shapes=[
            pltpu.VMEM((1, requests), jnp.int32),
            pltpu.VMEM((1, storage.shape[0]), jnp.int32),
            pltpu.VMEM((1, requests), jnp.int32),
            pltpu.VMEM(x.shape, BF16),
            pltpu.VMEM(base.shape, BF16),
            pltpu.VMEM(tk.shape, BF16),
            pltpu.VMEM(tv.shape, BF16),
            pltpu.VMEM((heads, requests, slots, head), BF16),
            pltpu.VMEM((heads, requests, slots, head), BF16),
            pltpu.VMEM((lanes, width), BF16),
            pltpu.VMEM((lanes, width), BF16),
            pltpu.VMEM((chunks, owners, TILE, width), BF16),
            pltpu.VMEM((chunks, owners, TILE, width), BF16),
            pltpu.VMEM((owners, 8, 128), F32),
            pltpu.VMEM((owners, 8, 128), F32),
            pltpu.VMEM((chunks, shards, owners * TILE // 2, 128), F32),
            pltpu.VMEM((chunks, owners, TILE, width), BF16),
            pltpu.VMEM((chunks, owners, TILE, width), BF16),
            dma((3,)),
            dma((6 + 2 * heads,)),
            dma((chunks, owners)),
            dma((chunks, owners)),
            dma((owners,)),
            dma((owners,)),
            dma((chunks, shards)),
            dma((chunks, shards)),
            dma((heads, chunks, owners)),
            dma((heads, chunks, owners)),
        ],
        compiler_params=pltpu.CompilerParams(
            collective_id=0, has_side_effects=True, vmem_limit_bytes=64 * 1024 * 1024
        ),
    )(
        adapter.reshape(1, requests), storage.reshape(1, -1), lengths.reshape(1, requests),
        x, base, tk, tv, k, v, down, up,
    )


def solution(mesh):
    rows = P(("groups", "inst"), "tp")
    cache = P(("groups", "inst"), "tp", None, None)
    in_specs = (
        rows, rows, rows, rows, cache, cache,
        P(("groups", "inst")),
        P(("groups", "inst")),
        P("groups"),
        P(("groups", "inst"), "tp", None),
        P(("groups", "inst"), None, "tp"),
    )
    step = functools.partial(body, mesh.shape["inst"], mesh.shape["tp"])
    return jax.shard_map(step, mesh=mesh, in_specs=in_specs, out_specs=rows, check_vma=False)
```

```python
import functools

import jax
import jax.numpy as jnp
from jax import lax
from jax.experimental import pallas as pl
from jax.experimental.pallas import tpu as pltpu
from jax.sharding import PartitionSpec as P

MESH = pl.DeviceIdType.MESH
F32 = jnp.float32
BF16 = jnp.bfloat16
TILE = 16
BLOCK = 8


def iota(shape, axis):
    return lax.broadcasted_iota(jnp.int32, shape, axis)


def to_column(row, count):
    shape = (count, row.shape[1])
    return jnp.sum(jnp.where(iota(shape, 0) == iota(shape, 1), row, 0.0), axis=1, keepdims=True)


def to_row(column):
    n = column.shape[0]
    return jnp.sum(jnp.where(iota((n, n), 0) == iota((n, n), 1), column, 0.0), axis=0, keepdims=True)


def kernel(
    owners, shards, chunks,
    adapter_hbm, storage_hbm, length_hbm,
    x_hbm, base_hbm, tk_hbm, tv_hbm, k_hbm, v_hbm, down_hbm, up_hbm,
    out_ref,
    adapter_ref, storage_ref, length_ref, x, base, tk, tv, kbuf, vbuf, down, up,
    snd, arr, tag_snd, tag_arr, part, delta, ret,
    index_sem, in_sem, snd_send, snd_recv, tag_send, tag_recv, part_send, part_recv, ret_send, ret_recv,
):
    me = lax.axis_index("inst")
    tp = lax.axis_index("tp")
    requests, width = x.shape
    heads = kbuf.shape[0]
    slots, head = kbuf.shape[2], kbuf.shape[3]
    span = width // heads
    group = span // head
    lanes = down.shape[0]
    rank = 64
    kept = lanes // rank
    rows = owners * TILE
    peer = lambda j: {"inst": lax.rem(me + j, owners)}
    mate = lambda j: {"tp": lax.rem(tp + j, shards)}

    index_loads = [
        pltpu.make_async_copy(adapter_hbm, adapter_ref, index_sem.at[0]),
        pltpu.make_async_copy(storage_hbm, storage_ref, index_sem.at[1]),
        pltpu.make_async_copy(length_hbm, length_ref, index_sem.at[2]),
    ]
    for load in index_loads:
        load.start()
    loads = [pltpu.make_async_copy(x_hbm, x, in_sem.at[0])]
    loads.append(pltpu.make_async_copy(down_hbm, down, in_sem.at[1]))
    loads.append(pltpu.make_async_copy(up_hbm, up, in_sem.at[2]))
    loads.append(pltpu.make_async_copy(base_hbm, base, in_sem.at[3]))
    loads.append(pltpu.make_async_copy(tk_hbm, tk, in_sem.at[4]))
    loads.append(pltpu.make_async_copy(tv_hbm, tv, in_sem.at[5]))
    for g in range(heads):
        loads.append(pltpu.make_async_copy(k_hbm.at[:, g], kbuf.at[g], in_sem.at[6 + 2 * g]))
        loads.append(pltpu.make_async_copy(v_hbm.at[:, g], vbuf.at[g], in_sem.at[7 + 2 * g]))
    for load in loads:
        load.start()

    barrier = pltpu.get_barrier_semaphore()
    for j in range(1, owners):
        pl.semaphore_signal(barrier, inc=1, device_id=peer(j), device_id_type=MESH)
    for j in range(1, shards):
        pl.semaphore_signal(barrier, inc=1, device_id=mate(j), device_id_type=MESH)

    catalog = storage_ref.shape[1]
    for load in index_loads:
        load.wait()
    adapter = to_column(adapter_ref[...].astype(F32), requests)
    stored = storage_ref[...].astype(F32)
    slot = jnp.sum(
        jnp.where(adapter == iota((requests, catalog), 1).astype(F32), stored, 0.0), axis=1, keepdims=True
    )
    home = jnp.floor((slot + 0.5) * (1.0 / kept))
    tag = slot - home * kept + 1.0
    home = home - me.astype(F32)
    home = jnp.where(home < 0.0, home + owners, home)
    home_row = to_row(home)
    square = (requests, requests)
    earlier = (home == home_row) & (iota(square, 1) < iota(square, 0))
    place = jnp.sum(jnp.where(earlier, 1.0, 0.0), axis=1, keepdims=True)
    turn = jnp.floor((place + 0.5) * (1.0 / TILE))
    spot = turn * rows + home * TILE + (place - turn * TILE)
    spot_row = to_row(spot)

    for j in range(owners):
        shape = (requests, 128)
        here = (home == float(j)) & (place == iota(shape, 1).astype(F32))
        line = jnp.sum(jnp.where(here, tag, 0.0), axis=0, keepdims=True)
        if j:
            tag_snd[j] = jnp.broadcast_to(line, (8, 128))
        else:
            tag_arr[0] = jnp.broadcast_to(line, (8, 128))

    loads[0].wait()
    own = []
    order = sorted(range(1, owners), key=lambda j: (abs(2 * j - owners), j))
    sends, row_sends = [], []
    for c in range(chunks):
        placing = (iota((rows, requests), 0).astype(F32) + float(c * rows) == spot_row)
        packed = jnp.dot(placing.astype(F32).astype(BF16), x[...], preferred_element_type=F32).astype(BF16)
        arr[c, 0] = packed[:TILE]
        snd[c] = packed.reshape(owners, TILE, width)
        if c == 0:
            pl.semaphore_wait(barrier, owners - 1 + shards - 1)
            for j in order:
                sends.append(pltpu.make_async_remote_copy(
                    src_ref=tag_snd.at[j], dst_ref=tag_arr.at[owners - j],
                    send_sem=tag_send.at[j], recv_sem=tag_recv.at[owners - j],
                    device_id=peer(j), device_id_type=MESH))
                sends[-1].start()
        ahead, row_sends = row_sends, []
        for i, j in enumerate(order):
            if ahead:
                ahead[i].wait_send()
            row_sends.append(pltpu.make_async_remote_copy(
                src_ref=snd.at[c, j], dst_ref=arr.at[c, owners - j],
                send_sem=snd_send.at[c, j], recv_sem=snd_recv.at[c, owners - j],
                device_id=peer(j), device_id_type=MESH))
            row_sends[-1].start()

    sends += row_sends

    def arrived(dst, sem, j, device):
        pltpu.make_async_remote_copy(
            src_ref=dst, dst_ref=dst, send_sem=sem, recv_sem=sem,
            device_id=device, device_id_type=MESH).wait_recv()

    pieces_of = lambda c: heads if c == chunks - 1 else 1
    half = rows // 2
    which = iota((rows, lanes), 1) // rank
    left = iota((half, 128), 1) < rank
    tags, back_sends = [], []
    for c in range(chunks):
        if c == 0:
            for j in range(1, owners):
                arrived(tag_arr.at[j], tag_recv.at[j], j, peer(j))
            loads[1].wait()
        columns = []
        for j in range(owners):
            shape = (TILE, 128)
            match = iota(shape, 1) == iota(shape, 0) + c * TILE
            columns.append(jnp.sum(jnp.where(match, tag_arr[j, 0:1, :], 0.0), axis=1, keepdims=True))
        mine = which.astype(F32) == jnp.concatenate(columns, axis=0) - 1.0
        tags.append(mine)
        for j in range(1, owners):
            arrived(arr.at[c, j], snd_recv.at[c, j], j, peer(j))
        product = lax.dot_general(
            arr[c].reshape(rows, width), down[...], (((1,), (1,)), ((), ())), preferred_element_type=F32
        )
        product = jnp.where(mine, product, 0.0)
        folded = product[:, :128]
        for a in range(1, lanes // 128):
            folded = folded + product[:, a * 128:(a + 1) * 128]
        folded = folded + pltpu.roll(folded, rank, 1)
        part[c, 0] = jnp.where(left, folded[:half], folded[half:])
        for j in range(1, shards):
            sends.append(pltpu.make_async_remote_copy(
                src_ref=part.at[c, 0], dst_ref=part.at[c, shards - j],
                send_sem=part_send.at[c, j], recv_sem=part_recv.at[c, shards - j],
                device_id=mate(j), device_id_type=MESH))
            sends[-1].start()
        for j in range(1, shards):
            arrived(part.at[c, j], part_recv.at[c, j], j, mate(j))
        total = part[c, 0]
        for j in range(1, shards):
            total = total + part[c, j]
        turned = pltpu.roll(total, rank, 1)
        low = jnp.concatenate([jnp.where(left, total, turned), jnp.where(left, turned, total)], axis=0)
        spread = jnp.where(mine, jnp.concatenate([low] * (lanes // 128), axis=1), 0.0).astype(BF16)
        if c == 0:
            loads[2].wait()
        pieces = pieces_of(c)
        columns = width // pieces
        for g in range(pieces):
            across = slice(g * columns, (g + 1) * columns)
            update = jnp.dot(spread, up[:, across], preferred_element_type=F32).astype(BF16)
            ret[c, 0, :, across] = update[:TILE]
            delta[c, :, :, across] = update.reshape(owners, TILE, columns)
            for j in order:
                back_sends.append(pltpu.make_async_remote_copy(
                    src_ref=delta.at[c, j, :, across], dst_ref=ret.at[c, owners - j, :, across],
                    send_sem=ret_send.at[g, c, j], recv_sem=ret_recv.at[g, c, owners - j],
                    device_id=peer(j), device_id_type=MESH))
                back_sends[-1].start()

    scale = head ** (-0.5)
    spots = chunks * rows
    undo = (iota((requests, spots), 1).astype(F32) == spot).astype(F32).astype(BF16)
    length = to_column(length_ref[...].astype(F32), requests)
    deep = BLOCK * group
    wide = BLOCK * slots
    request = iota((deep, 1), 0) % BLOCK
    beside = max(1, 128 // slots)
    lane_tile = beside * slots
    holds = [request // beside == t for t in range(wide // lane_tile)]
    upper = request >= BLOCK // 2
    blocks = range(0, requests, BLOCK)

    def in_rows(values):
        return jnp.concatenate([values[r:r + BLOCK] for r in blocks for _ in range(group)], axis=0)

    def beside_halves(cache, g, r):
        middle = r + BLOCK // 2
        return jnp.concatenate(
            [cache[g, r:middle].reshape(-1, head), cache[g, middle:middle + BLOCK // 2].reshape(-1, head)], axis=1
        )

    first = (iota((requests * group, 1), 0) % beside) * slots
    last = first + in_rows(length).astype(jnp.int32)
    where_slot = iota((requests * group, lane_tile), 1)
    valid = (where_slot >= first) & (where_slot < last)
    for load in loads[3:6]:
        load.wait()
    early = base[...].astype(F32)
    for c in range(chunks - 1):
        for j in range(1, owners):
            arrived(ret.at[c, j], ret_recv.at[0, c, j], j, peer(j))
        early = early + jnp.dot(
            undo[:, c * rows:(c + 1) * rows], ret[c].reshape(rows, width), preferred_element_type=F32)
    for g in range(heads):
        loads[6 + 2 * g].wait()
        loads[7 + 2 * g].wait()
        for c in range(chunks - 1, chunks):
            pieces = pieces_of(c)
            if g < pieces:
                across = slice(g * (width // pieces), (g + 1) * (width // pieces))
                for j in range(1, owners):
                    arrived(ret.at[c, j, :, across], ret_recv.at[g, c, j], j, peer(j))
        fixed = early[:, g * span:(g + 1) * span]
        correction = fixed + jnp.dot(
            undo[:, spots - rows:], ret[chunks - 1, :, :, g * span:(g + 1) * span].reshape(rows, span),
            preferred_element_type=F32)
        query = correction.astype(BF16).astype(F32)
        fresh_key = tk[:, g * head:(g + 1) * head].astype(F32)
        fresh_value = tv[:, g * head:(g + 1) * head].astype(F32)
        queries, folded = [], []
        for r in blocks:
            q = jnp.concatenate([query[r:r + BLOCK, h * head:(h + 1) * head] for h in range(group)], axis=0)
            queries.append(q)
            every = lax.dot_general(
                q.astype(BF16), kbuf[g, r:r + BLOCK].reshape(wide, head), (((1,), (1,)), ((), ())),
                preferred_element_type=F32,
            )
            scores = every[:, :lane_tile]
            for t in range(1, len(holds)):
                scores = jnp.where(holds[t], every[:, t * lane_tile:(t + 1) * lane_tile], scores)
            folded.append(scores)
        scores = jnp.where(valid, jnp.concatenate(folded, axis=0) * scale, -1e30)
        fresh = jnp.sum(jnp.concatenate(queries, axis=0) * in_rows(fresh_key), axis=1, keepdims=True) * scale
        top = jnp.maximum(jnp.max(scores, axis=1, keepdims=True), fresh)
        expo = jnp.exp(scores - top)
        expo_new = jnp.exp(fresh - top)
        inverse = 1.0 / (jnp.sum(expo, axis=1, keepdims=True) + expo_new)
        weights = expo * inverse
        added = (expo_new * inverse).astype(BF16).astype(F32) * in_rows(fresh_value)
        outs = []
        for i, r in enumerate(blocks):
            here = slice(i * deep, (i + 1) * deep)
            spread = jnp.concatenate([jnp.where(hold, weights[here], 0.0) for hold in holds], axis=1)
            mixed = jnp.dot(spread.astype(BF16), vbuf[g, r:r + BLOCK].reshape(wide, head), preferred_element_type=F32)
            outs.append(mixed + added[here])
        for i in range(0, len(blocks), 2):
            for h in range(group):
                piece = slice(h * BLOCK, (h + 1) * BLOCK)
                out_ref[blocks[i]:blocks[i] + 2 * BLOCK, g * span + h * head:g * span + (h + 1) * head] = (
                    jnp.concatenate([outs[i][piece], outs[i + 1][piece]], axis=0).astype(BF16)
                )
    for send in sends + back_sends:
        send.wait_send()


def body(owners, shards, x, base, tk, tv, k, v, lengths, adapter, storage, down, up):
    requests, width = x.shape
    heads, slots, head = k.shape[1:]
    kept, _, rank = down.shape
    capacity = max(2, 2 * requests // owners)
    chunks = -(-capacity // TILE)
    span = width // heads
    lanes = kept * rank
    down = jnp.swapaxes(down, 1, 2).reshape(lanes, width)
    up = up.reshape(lanes, width)
    large = pl.BlockSpec(memory_space=pltpu.HBM)
    dma = pltpu.SemaphoreType.DMA
    return pl.pallas_call(
        functools.partial(kernel, owners, shards, chunks),
        out_shape=jax.ShapeDtypeStruct((requests, width), BF16),
        in_specs=[large] * 11,
        out_specs=pl.BlockSpec(memory_space=pltpu.VMEM),
        scratch_shapes=[
            pltpu.VMEM((1, requests), jnp.int32),
            pltpu.VMEM((1, storage.shape[0]), jnp.int32),
            pltpu.VMEM((1, requests), jnp.int32),
            pltpu.VMEM(x.shape, BF16),
            pltpu.VMEM(base.shape, BF16),
            pltpu.VMEM(tk.shape, BF16),
            pltpu.VMEM(tv.shape, BF16),
            pltpu.VMEM((heads, requests, slots, head), BF16),
            pltpu.VMEM((heads, requests, slots, head), BF16),
            pltpu.VMEM((lanes, width), BF16),
            pltpu.VMEM((lanes, width), BF16),
            pltpu.VMEM((chunks, owners, TILE, width), BF16),
            pltpu.VMEM((chunks, owners, TILE, width), BF16),
            pltpu.VMEM((owners, 8, 128), F32),
            pltpu.VMEM((owners, 8, 128), F32),
            pltpu.VMEM((chunks, shards, owners * TILE // 2, 128), F32),
            pltpu.VMEM((chunks, owners, TILE, width), BF16),
            pltpu.VMEM((chunks, owners, TILE, width), BF16),
            dma((3,)),
            dma((6 + 2 * heads,)),
            dma((chunks, owners)),
            dma((chunks, owners)),
            dma((owners,)),
            dma((owners,)),
            dma((chunks, shards)),
            dma((chunks, shards)),
            dma((heads, chunks, owners)),
            dma((heads, chunks, owners)),
        ],
        compiler_params=pltpu.CompilerParams(
            collective_id=0, has_side_effects=True, vmem_limit_bytes=64 * 1024 * 1024
        ),
    )(
        adapter.reshape(1, requests), storage.reshape(1, -1), lengths.reshape(1, requests),
        x, base, tk, tv, k, v, down, up,
    )


def solution(mesh):
    rows = P(("groups", "inst"), "tp")
    cache = P(("groups", "inst"), "tp", None, None)
    in_specs = (
        rows, rows, rows, rows, cache, cache,
        P(("groups", "inst")),
        P(("groups", "inst")),
        P("groups"),
        P(("groups", "inst"), "tp", None),
        P(("groups", "inst"), None, "tp"),
    )
    step = functools.partial(body, mesh.shape["inst"], mesh.shape["tp"])
    return jax.shard_map(step, mesh=mesh, in_specs=in_specs, out_specs=rows, check_vma=False)
```
